256 devices in a mesh: expert: 64 (over y, z, core), tensor: 4 (over x).
Axes of the slice: x: 4, y: 4, z: 8, core: 2. Of those that a mesh axis runs over, the one named last changes fastest.
Arguments:
- hidden: bfloat16 [1024, 4096], P('expert'), may hold values from -90 to 90
- norm_gain: float32 [4, 4096], replicated, may hold values from 0.5 to 1.5
- head_weight: bfloat16 [4096, 4, 64128], P(None, 'tensor', 'expert'), may hold values from -8 to 8
- expert_ids: int32 [1024, 2], P('expert'), may hold values from 0 to 3, as said below
- mix_weight: int32 [1024, 2], P('expert'), may hold values from 1 to 65535
Outputs:
- mixed_logprob: float32 [1024, 64128], P('expert', 'tensor')
The draws below stay inside these ranges and needn't reach their ends.
Inputs may be any that keep to these rules, and one draw needn't show every extreme that they name: `expert_ids`: each row names 2 different experts. Among the 16 rows of each index of expert, one expert, the same for every index and drawn from the seed, is named by exactly 15 rows, and no expert by more than 15 rows.
All inputs are finite; a program needn't handle non-finite values.
Results may differ from the reference program's by a relative error of at most 0.00063.
Values may be sent and summed in bfloat16 or wider, within the bound.
A program may use at most 128 MiB of HBM per device.

```python
import math
import jax
import jax.numpy as jnp
from jax import lax

D = 4096
VOCAB = 64128
EXPERTS = 4
TOP = 2
TOK_DEV = 16
ROWS = 1024
MOST = 15
VQ = 16032


def draw_hidden(key, part):
    key = jax.random.fold_in(key, 1)
    keys = jax.random.split(key, 1)
    base_draw = jnp.clip(jax.random.normal(keys[0], (ROWS, D), jnp.float32), -6.0, 6.0)
    row_values = base_draw
    return row_values.astype(jnp.bfloat16)


def draw_head_weight(key, part):
    key = jax.random.fold_in(key, 2)
    keys = jax.random.split(key, 1)
    quarters = VOCAB // VQ
    base_draw = jnp.clip(jax.random.normal(keys[0], (D, quarters, EXPERTS * VQ), jnp.float32), -6.0, 6.0)
    weights = 3.0 * base_draw / math.sqrt(D)
    return weights.astype(jnp.bfloat16)


def draw_expert_ids(key, part):
    key = jax.random.fold_in(key, 3)
    keys = jax.random.split(key, 5)
    blocks = ROWS // TOK_DEV
    hot_expert = jax.random.randint(keys[0], (), 0, EXPERTS).astype(jnp.int32)
    cold_experts = ((hot_expert + 1 + jnp.arange(EXPERTS - 1, dtype=jnp.int32)) % EXPERTS).astype(jnp.int32)
    partner = cold_experts[jax.random.randint(keys[1], (blocks, MOST), 0, EXPERTS - 1)]
    counts = jnp.sum((partner[:, :, None] == cold_experts[None, None, :]).astype(jnp.int32), axis=1)
    scores = counts * 4 + jnp.arange(EXPERTS - 1, dtype=jnp.int32)[None, :]
    ranked = jnp.argsort(scores, axis=1, stable=True)
    lone_pair = cold_experts[ranked[:, :2]]
    hot_rows = jnp.stack([jnp.full((blocks, MOST), hot_expert, jnp.int32), partner], axis=-1)
    flipped = jax.random.randint(keys[2], (blocks, MOST), 0, 2)
    hot_rows = jnp.where((flipped == 1)[:, :, None], hot_rows[:, :, ::-1], hot_rows)
    lone_flip = jax.random.randint(keys[3], (blocks,), 0, 2)
    lone_pair = jnp.where((lone_flip == 1)[:, None], lone_pair[:, ::-1], lone_pair)
    block_rows = jnp.concatenate([hot_rows, lone_pair[:, None, :]], axis=1)
    shuffle = jax.vmap(lambda sub_key: jax.random.permutation(sub_key, TOK_DEV))(jax.random.split(keys[4], blocks))
    block_rows = jnp.take_along_axis(block_rows, shuffle[:, :, None].astype(jnp.int32), axis=1)
    return block_rows.reshape(ROWS, TOP).astype(jnp.int32)


def touch_ends(drawn, rng, smallest, largest):
    extent = drawn.shape
    spot = [jax.random.randint(jax.random.fold_in(rng, axis), (), 0, extent[axis]) for axis in range(len(extent))]
    drawn = drawn.at[tuple(spot)].set(smallest)
    longest = extent.index(max(extent))
    spot[longest] = (spot[longest] + 1) % extent[longest]
    return drawn.at[tuple(spot)].set(largest)


def setup_inputs(seed: int = 0) -> dict:
    arg_keys = jax.random.split(jax.random.key(seed), 6)
    hidden = draw_hidden(jax.random.fold_in(arg_keys[5], 71), 0)
    norm_gain = jnp.clip(1.0 + 0.1 * jax.random.normal(arg_keys[1], (EXPERTS, D), jnp.float32), 0.5, 1.5)
    head_weight = draw_head_weight(jax.random.fold_in(arg_keys[5], 71), 0)
    expert_ids = draw_expert_ids(jax.random.fold_in(arg_keys[5], 71), 0)
    mix_weight = touch_ends(jax.random.randint(arg_keys[4], (ROWS, TOP), 1, 65536), jax.random.fold_in(arg_keys[4], 1), 1, 65535).astype(jnp.int32)
    return {"hidden": hidden, "norm_gain": norm_gain, "head_weight": head_weight, "expert_ids": expert_ids, "mix_weight": mix_weight}


EPS = 1e-05

def reference(hidden, norm_gain, head_weight, expert_ids, mix_weight):
    quarters = head_weight.shape[1]
    head_table = head_weight.reshape(D, quarters, EXPERTS, VQ)
    counts = mix_weight.astype(jnp.float32)
    shares = counts / lax.optimization_barrier(jnp.sum(counts, axis=1, keepdims=True))
    hidden_f32 = hidden.astype(jnp.float32)
    rms_scale = jnp.sqrt(lax.optimization_barrier(jnp.mean(hidden_f32 * hidden_f32, axis=1, keepdims=True)) + EPS)
    mixture = jnp.zeros((ROWS, VOCAB), jnp.float32)
    for expert in range(EXPERTS):
        normed = (hidden_f32 / rms_scale * norm_gain[expert]).astype(jnp.bfloat16)
        matrix = head_table[:, :, expert, :].reshape(D, VOCAB)
        logits = jnp.dot(normed, matrix, preferred_element_type=jnp.float32)
        row_top = lax.optimization_barrier(jnp.max(logits, axis=1, keepdims=True))
        raised = jnp.exp(logits - row_top)
        probs = (raised / lax.optimization_barrier(jnp.sum(raised, axis=1, keepdims=True))).astype(jnp.bfloat16)
        share_col = lax.optimization_barrier(jnp.sum(jnp.where(expert_ids == expert, shares, jnp.float32(0.0)), axis=1, keepdims=True))
        mixture = mixture + share_col * probs.astype(jnp.float32)
    return jnp.log(mixture)
```

```python
import jax
import jax.numpy as jnp
from jax import lax
from jax.experimental import pallas as pl
from jax.experimental.pallas import tpu as pltpu
from jax.sharding import PartitionSpec as P

EPS = 1e-05
FAR = -1e30
NX, NY, NZ, NC = 4, 4, 8, 2
ROWS_DEV = 16
D = 4096
FQ = D // NX
VD = 1002
VP = 1024
FA = 640
FB = FQ - FA
MESH = pl.DeviceIdType.MESH
F32 = jnp.float32
BF16 = jnp.bfloat16

SLOT = {0: 0, 7: 1, 1: 2, 6: 3, 2: 4, 5: 5, 3: 6, 4: 7}
DZ = {s: d for d, s in SLOT.items()}


def sem_table():
    names = []
    names += [("y", k) for k in range(1, NY)]
    names += [("sy", k) for k in range(1, NY)]
    names += [("sz", dz, dc) for dz in range(NZ) for dc in range(NC) if (dz, dc) != (0, 0)]
    names += [("az", dz) for dz in range(1, NZ)]
    names += [("ax", dz, dx) for dz in range(NZ) for dx in range(1, NX)]
    names += [("bx", dx) for dx in range(1, NX)]
    names += [("bz", dz, dx) for dz in range(1, NZ) for dx in range(NX)]
    names += [("cc", dz, dx) for dz in range(NZ) for dx in range(NX)]
    names += [("tx", dx, dc) for dx in range(NX) for dc in range(NC) if (dx, dc) != (0, 0)]
    names += [("tz", dz) for dz in range(1, NZ)]
    names += [(kind, sign, q) for kind in ("far", "near", "sum") for sign in (1, -1) for q in range(2)]
    names += [("rz", dz, dc) for dz in range(NZ) for dc in range(NC) if (dz, dc) != (0, 0)]
    return {name: i for i, name in enumerate(names)}


SEMS = sem_table()


def body(h_ref, g_ref, ids_ref, mw_ref, w_ref, out_ref,
         wt, n4, gat, sh_src, sh_y, sh_all, lg, mcol, st_own, st_x, st_zsrc, st_z,
         fm, fs, cm, cf, pr, far_in, near_in, sum_in, mix, w_sem, loc_sem, ss, rs):
    me = lax.axis_index("expert")
    x = lax.axis_index("tensor")
    y = me // (NZ * NC)
    z = (me // NC) % NZ
    c = me % NC

    def dev(dx=0, dy=0, dz=0, dc=0):
        yy = (y + dy) % NY
        zz = (z + dz) % NZ
        cc = (c + dc) % NC
        return ((yy * NZ + zz) * NC + cc, (x + dx) % NX)

    sent = []

    def send(key, src, dst, to):
        k = SEMS[key]
        copy = pltpu.make_async_remote_copy(
            src_ref=src, dst_ref=dst, send_sem=ss.at[k], recv_sem=rs.at[k],
            device_id=to, device_id_type=MESH)
        copy.start()
        sent.append(copy)

    def arrive(key, dst):
        k = SEMS[key]
        pltpu.make_async_remote_copy(
            src_ref=dst, dst_ref=dst, send_sem=ss.at[k], recv_sem=rs.at[k],
            device_id=dev(dc=1), device_id_type=MESH).wait_recv()

    w_copy = pltpu.make_async_copy(w_ref, wt, w_sem)
    w_copy.start()

    peers = [dev(dy=k) for k in range(1, NY)]
    peers += [dev(dz=a, dc=b) for a in range(NZ) for b in range(NC) if (a, b) != (0, 0)]
    peers += [dev(dx=a, dc=b) for a in range(1, NX) for b in range(NC)]
    barrier = pltpu.get_barrier_semaphore()
    for peer in peers:
        pl.semaphore_signal(barrier, inc=1, device_id=peer, device_id_type=MESH)

    h_all = h_ref[...].astype(F32)
    rms = jnp.sqrt(jnp.mean(h_all * h_all, axis=1, keepdims=True) + EPS)
    cols = pl.ds(pl.multiple_of(x * FQ, FQ), FQ)
    h_q = h_ref[:, cols].astype(F32) / rms
    for e in range(NY):
        n4[e] = (h_q * g_ref[pl.ds(e, 1), cols]).astype(BF16)
    counts = mw_ref[...].astype(F32)
    shares = counts / (counts[:, 0:1] + counts[:, 1:2])
    ids = ids_ref[...]
    lane = lax.broadcasted_iota(jnp.int32, (ROWS_DEV, 128), 1)
    row = lax.broadcasted_iota(jnp.int32, (ROWS_DEV, 128), 0)
    mine = lane - row == c * 64 + y * ROWS_DEV
    for e in range(NY):
        col = jnp.sum(jnp.where(ids == e, shares, 0.0), axis=1, keepdims=True)
        line = jnp.sum(jnp.where(mine, col, 0.0), axis=0, keepdims=True)
        sh_src[e] = jnp.broadcast_to(line, (8, 128))

    pl.semaphore_wait(barrier, len(peers))

    for k in (2, 1, 3):
        send(("y", k), n4.at[(y + k) % NY], gat.at[0, x, c, y], dev(dy=k))
    for k in (2, 1, 3):
        send(("sy", k), sh_src.at[(y + k) % NY], sh_y.at[k], dev(dy=k))
    own = pltpu.make_async_copy(n4.at[y], gat.at[0, x, c, y], loc_sem)
    own.start()
    own.wait()
    for k in (1, 3, 2):
        arrive(("y", k), gat.at[0, x, c, (y - k) % NY])

    def unit(dz, dx):
        return gat.at[SLOT[dz], (x + dx) % NX, c]

    def part_a(dz, dx):
        return gat.at[SLOT[dz], (x + dx) % NX, c, :, :, pl.ds(0, FA)]

    def part_b(dz, dx):
        return gat.at[SLOT[dz], (x + dx) % NX, c, :, :, pl.ds(FA, FB)]

    def a_along_z(dz, step):
        to = (dz - step) % NZ
        send(("az", to), part_a(dz, 0), part_a(to, 0), dev(dz=step))

    def a_along_x(dz):
        send(("ax", dz, 3), part_a(dz, 0), part_a(dz, 0), dev(dx=1))
        send(("ax", dz, 1), part_a(dz, 0), part_a(dz, 0), dev(dx=-1))

    def a_opposite(dz):
        for dx in (3, 1):
            arrive(("ax", dz, dx), part_a(dz, dx))
            if dx == (3 if dz % 2 == 0 else 1):
                step = 1 if dx == 3 else -1
                send(("ax", dz, 2), part_a(dz, dx), part_a(dz, dx), dev(dx=step))

    def b_along_z(dz, dx, step):
        to = (dz - step) % NZ
        send(("bz", to, dx), part_b(dz, dx), part_b(to, dx), dev(dz=step))

    def to_sibling(dz, dx):
        send(("cc", dz, dx), unit(dz, dx), unit(dz, dx), dev(dc=1))

    def right_hops(dx):
        return 4 if dx in (0, 1) else 3

    def b_round(k, dx):
        if k <= right_hops(dx):
            arrive(("bz", NZ - k, dx), part_b(NZ - k, dx))
            if k < right_hops(dx):
                b_along_z(NZ - k, dx, 1)
        if k <= 7 - right_hops(dx):
            arrive(("bz", k, dx), part_b(k, dx))
            if k < 7 - right_hops(dx):
                b_along_z(k, dx, -1)

    def logits(g):
        rows = 2 * 128

        def tile(n, carry):
            vocab = pl.ds(pl.multiple_of(n * 256, 256), 256)
            acc = jnp.zeros((rows, 256), F32)
            for xi in range(NX):
                lhs = gat[2 * g:2 * g + 2, xi].reshape(rows, FQ)
                acc += lax.dot_general(
                    lhs, wt[vocab, xi * FQ:(xi + 1) * FQ],
                    (((1,), (1,)), ((), ())), preferred_element_type=F32)
            lg[g * rows:(g + 1) * rows, vocab] = acc
            return carry

        lax.fori_loop(0, 3, tile, 0)
        acc = jnp.zeros((rows, VD - 768), F32)
        for xi in range(NX):
            lhs = gat[2 * g:2 * g + 2, xi].reshape(rows, FQ)
            acc += lax.dot_general(
                lhs, wt[768:VD, xi * FQ:(xi + 1) * FQ],
                (((1,), (1,)), ((), ())), preferred_element_type=F32)
        lg[g * rows:(g + 1) * rows, 768:VP] = jnp.concatenate(
            [acc, jnp.full((rows, VP - VD), FAR, F32)], axis=1)

        def stat(i, carry):
            at = pl.ds(pl.multiple_of(g * rows + i * 32, 32), 32)
            block = lg[at, :]
            top = jnp.max(block, axis=1, keepdims=True)
            total = jnp.sum(jnp.exp(block - top), axis=1, keepdims=True)
            mcol[0, at, :] = jnp.broadcast_to(top, (32, 128))
            mcol[1, at, :] = jnp.broadcast_to(total, (32, 128))
            return carry

        lax.fori_loop(0, rows // 32, stat, 0)
        for s in (2 * g, 2 * g + 1):
            at = (z + DZ[s]) % NZ
            for j in range(2):
                st_own[pl.ds(j * 8 + at, 1), :] = jnp.sum(
                    jnp.where(eye(), mcol[j, s * 128:(s + 1) * 128, :], 0.0), axis=0, keepdims=True)

    def eye():
        return (lax.broadcasted_iota(jnp.int32, (128, 128), 0)
                == lax.broadcasted_iota(jnp.int32, (128, 128), 1))

    a_along_z(0, 1)
    a_along_z(0, -1)
    send(("bx", 3), part_b(0, 0), part_b(0, 0), dev(dx=1))
    send(("bx", 1), part_b(0, 0), part_b(0, 0), dev(dx=-1))
    a_along_x(0)
    b_along_z(0, 0, 1)
    b_along_z(0, 0, -1)
    to_sibling(0, 0)

    for k in (1, 3, 2):
        arrive(("sy", k), sh_y.at[k])
    sh_all[0, c] = sh_src[y] + sh_y[1] + sh_y[2] + sh_y[3]
    for dz in range(NZ):
        for dc in range(NC):
            if (dz, dc) != (0, 0):
                send(("sz", (-dz) % NZ, dc), sh_all.at[0, c], sh_all.at[(-dz) % NZ, c],
                     dev(dz=dz, dc=dc))

    for dx in (3, 1, 2):
        arrive(("bx", dx), part_b(0, dx))
        if dx == 3:
            send(("bx", 2), part_b(0, 3), part_b(0, 3), dev(dx=1))
        b_along_z(0, dx, 1)
        b_along_z(0, dx, -1)

    def finish_x(dz):
        for dx in range(1, NX):
            if dx == 2:
                arrive(("ax", dz, 2), part_a(dz, 2))
            to_sibling(dz, dx)

    def from_sibling(dz):
        for dx in range(NX):
            arrive(("cc", dz, dx), gat.at[SLOT[dz], (x + dx) % NX, 1 - c])

    for k in range(1, 5):
        arrive(("az", NZ - k), part_a(NZ - k, 0))
        if k < 4:
            a_along_z(NZ - k, 1)
        a_along_x(NZ - k)
        if k < 4:
            arrive(("az", k), part_a(k, 0))
            if k < 3:
                a_along_z(k, -1)
            a_along_x(k)
        if k == 1:
            a_opposite(0)
        else:
            a_opposite(NZ - k + 1)
            a_opposite(k - 1)
        for dx in range(NX):
            b_round(k, dx)
        if k < 4:
            to_sibling(NZ - k, 0)
            to_sibling(k, 0)
        else:
            to_sibling(4, 0)
        if k == 1:
            finish_x(0)
            w_copy.wait()
        else:
            finish_x(NZ - k + 1)
            finish_x(k - 1)
        if k == 2:
            from_sibling(0)
            from_sibling(7)
            logits(0)
        if k == 3:
            from_sibling(1)
            from_sibling(6)
            logits(1)
    a_opposite(4)
    finish_x(4)
    from_sibling(2)
    from_sibling(5)
    logits(2)
    from_sibling(3)
    from_sibling(4)
    logits(3)

    def merge(parts):
        top = parts[0][0]
        for m, _ in parts[1:]:
            top = jnp.maximum(top, m)
        total = jnp.zeros_like(top)
        for m, s in parts:
            total += s * jnp.exp(m - top)
        return top, total

    near_peers = [(a, b) for a in range(NX) for b in range(NC) if (a, b) != (0, 0)]
    for a, b in near_peers:
        send(("tx", (-a) % NX, b), st_own, st_x.at[(-a) % NX, b], dev(dx=a, dc=b))
    parts = [(st_own[0:8], st_own[8:16])]
    for a, b in near_peers:
        arrive(("tx", a, b), st_x.at[a, b])
        parts.append((st_x[a, b, 0:8], st_x[a, b, 8:16]))
    top, total = merge(parts)
    st_zsrc[0:8] = top
    st_zsrc[8:16] = total
    for k in range(1, NZ):
        send(("tz", (-k) % NZ), st_zsrc, st_z.at[(-k) % NZ], dev(dz=k))
    for dz in range(NZ):
        for dc in range(NC):
            if (dz, dc) != (0, 0):
                arrive(("sz", dz, dc), sh_all.at[dz, (c + dc) % NC])
    parts = [(top, total)]
    for k in range(1, NZ):
        arrive(("tz", k), st_z.at[k])
        parts.append((st_z[k, 0:8], st_z[k, 8:16]))
    top, total = merge(parts)
    fm[...] = top
    fs[...] = total

    for s in range(NZ):
        at = (z + DZ[s]) % NZ
        share = sh_all[DZ[s], 0, 0:1] + sh_all[DZ[s], 1, 0:1]
        m_line = fm[pl.ds(at, 1), :]
        f_line = share / fs[pl.ds(at, 1), :]
        m_c = jnp.sum(jnp.where(eye(), m_line, 0.0), axis=1, keepdims=True)
        f_c = jnp.sum(jnp.where(eye(), f_line, 0.0), axis=1, keepdims=True)
        cm[s * 128:(s + 1) * 128, :] = jnp.broadcast_to(m_c, (128, 128))
        cf[s * 128:(s + 1) * 128, :] = jnp.broadcast_to(f_c, (128, 128))

    def weigh(t):
        def step(i, carry):
            r0 = pl.multiple_of(i * 64 + t * ROWS_DEV, ROWS_DEV)
            at = pl.ds(r0, ROWS_DEV)
            block = lg[at, :].reshape(ROWS_DEV, VP)
            m = cm[at, 0:1]
            f = cf[at, 0:1]
            pr[t, i // NC, i % NC] = (jnp.exp(block - m) * f).astype(BF16)
            return carry

        lax.fori_loop(0, NZ * NC, step, 0)

    def half(ref, h, q):
        return ref.at[pl.ds(h * 4 + q * 2, 2)]

    ahead, behind, across = (y + 1) % NY, (y + 3) % NY, (y + 2) % NY
    weigh(across)
    for q in range(2):
        send(("far", 1, q), half(pr.at[across], 1, q), far_in.at[0, q], dev(dy=1))
        send(("far", -1, q), half(pr.at[across], 0, q), far_in.at[1, q], dev(dy=-1))
    weigh(ahead)
    for q in range(2):
        send(("near", 1, q), half(pr.at[ahead], 0, q), near_in.at[0, q], dev(dy=1))
    weigh(behind)
    for q in range(2):
        send(("near", -1, q), half(pr.at[behind], 1, q), near_in.at[1, q], dev(dy=-1))
    for q in range(2):
        for sign, t, h, j in ((1, ahead, 1, 0), (-1, behind, 0, 1)):
            arrive(("far", sign, q), far_in.at[j, q])

            def add(i, carry, t=t, h=h, j=j, q=q):
                s = h * 4 + q * 2 + i // NC
                pr[t, s, i % NC] = (pr[t, s, i % NC].astype(F32)
                                    + far_in[j, q, i // NC, i % NC].astype(F32)).astype(BF16)
                return carry

            lax.fori_loop(0, 2 * NC, add, 0)
            send(("sum", sign, q), half(pr.at[t], h, q), sum_in.at[j, q], dev(dy=sign))
    weigh(y)
    for q in range(2):
        for h in range(2):
            near_key, near_j = (("near", 1, q), 0) if h == 0 else (("near", -1, q), 1)
            sum_key, sum_j = (("sum", -1, q), 1) if h == 0 else (("sum", 1, q), 0)
            arrive(near_key, near_in.at[near_j, q])
            arrive(sum_key, sum_in.at[sum_j, q])

            def add(i, carry, h=h, q=q, near_j=near_j, sum_j=sum_j):
                s = h * 4 + q * 2 + i // NC
                mix[s, i % NC] = (pr[y, s, i % NC].astype(F32)
                                  + near_in[near_j, q, i // NC, i % NC].astype(F32)
                                  + sum_in[sum_j, q, i // NC, i % NC].astype(F32)).astype(BF16)
                return carry

            lax.fori_loop(0, 2 * NC, add, 0)
            for i in range(2):
                s = h * 4 + q * 2 + i
                for dc in range(NC):
                    if (s, dc) != (0, 0):
                        dz = DZ[s]
                        send(("rz", (-dz) % NZ, dc), mix.at[s, (c + dc) % NC],
                             out_ref.at[z, c], dev(dz=dz, dc=dc))
    last = pltpu.make_async_copy(mix.at[0, c], out_ref.at[z, c], loc_sem)
    last.start()
    last.wait()
    for dz in range(NZ):
        for dc in range(NC):
            if (dz, dc) != (0, 0):
                arrive(("rz", dz, dc), out_ref.at[(z + dz) % NZ, (c + dc) % NC])
    for copy in sent:
        copy.wait_send()


def spread(mix_ref, out_ref):
    chunks = NZ * NC
    for j in range(chunks):
        start = j * VD
        base, shift = start // 128 * 128, start % 128
        vals = jnp.log(mix_ref[j // NC, j % NC].astype(F32))
        wide = jnp.concatenate([vals, jnp.zeros((ROWS_DEV, 128), F32)], axis=1)
        if shift:
            wide = pltpu.roll(wide, shift, 1)
            lane = lax.broadcasted_iota(jnp.int32, (ROWS_DEV, 128), 1)
            first = jnp.where(lane < shift, out_ref[:, base:base + 128], wide[:, 0:128])
            out_ref[:, base:base + 128] = first
        else:
            out_ref[:, base:base + 128] = wide[:, 0:128]
        end = min(base + wide.shape[1], chunks * VD)
        out_ref[:, base + 128:end] = wide[:, 128:end - base]


def per_device(hidden, norm_gain, head_weight, expert_ids, mix_weight):
    wt_in = jnp.transpose(head_weight.reshape(D, VD))
    vmem = pl.BlockSpec(memory_space=pltpu.VMEM)
    n_sem = len(SEMS)
    returned = pl.pallas_call(
        body,
        out_shape=jax.ShapeDtypeStruct((NZ, NC, ROWS_DEV, VP), BF16),
        in_specs=[vmem, vmem, vmem, vmem, pl.BlockSpec(memory_space=pl.ANY)],
        out_specs=vmem,
        scratch_shapes=[
            pltpu.VMEM((VD, D), BF16),
            pltpu.VMEM((NY, ROWS_DEV, FQ), BF16),
            pltpu.VMEM((NZ, NX, NC, NY, ROWS_DEV, FQ), BF16),
            pltpu.VMEM((NY, 8, 128), F32),
            pltpu.VMEM((NY, 8, 128), F32),
            pltpu.VMEM((NZ, NC, 8, 128), F32),
            pltpu.VMEM((NZ * 128, VP), F32),
            pltpu.VMEM((2, NZ * 128, 128), F32),
            pltpu.VMEM((16, 128), F32),
            pltpu.VMEM((NX, NC, 16, 128), F32),
            pltpu.VMEM((16, 128), F32),
            pltpu.VMEM((NZ, 16, 128), F32),
            pltpu.VMEM((8, 128), F32),
            pltpu.VMEM((8, 128), F32),
            pltpu.VMEM((NZ * 128, 128), F32),
            pltpu.VMEM((NZ * 128, 128), F32),
            pltpu.VMEM((NY, NZ, NC, ROWS_DEV, VP), BF16),
            pltpu.VMEM((2, 2, 2, NC, ROWS_DEV, VP), BF16),
            pltpu.VMEM((2, 2, 2, NC, ROWS_DEV, VP), BF16),
            pltpu.VMEM((2, 2, 2, NC, ROWS_DEV, VP), BF16),
            pltpu.VMEM((NZ, NC, ROWS_DEV, VP), BF16),
            pltpu.SemaphoreType.DMA,
            pltpu.SemaphoreType.DMA,
            pltpu.SemaphoreType.DMA((n_sem,)),
            pltpu.SemaphoreType.DMA((n_sem,)),
        ],
        compiler_params=pltpu.CompilerParams(
            collective_id=0, has_side_effects=True, vmem_limit_bytes=56 * 1024 * 1024),
    )(hidden, norm_gain, expert_ids, mix_weight, wt_in)
    return pl.pallas_call(
        spread,
        out_shape=jax.ShapeDtypeStruct((ROWS_DEV, NZ * NC * VD), F32),
        in_specs=[vmem],
        out_specs=vmem,
    )(returned)


def solution(mesh):
    placed = (
        P("expert", None),
        P(),
        P(None, "tensor", "expert"),
        P("expert", None),
        P("expert", None),
    )
    return jax.shard_map(
        per_device, mesh=mesh, in_specs=placed, out_specs=P("expert", "tensor"), check_vma=False
    )
```

```python
import jax
import jax.numpy as jnp
from jax import lax
from jax.experimental import pallas as pl
from jax.experimental.pallas import tpu as pltpu
from jax.sharding import PartitionSpec as P

EPS = 1e-05
FAR = -1e30
LOG2E = 1.4426950408889634
NX, NY, NZ, NC = 4, 4, 8, 2
ROWS_DEV = 16
D = 4096
FQ = D // NX
VD = 1002
VP = 1024
FA = 640
FB = FQ - FA
MESH = pl.DeviceIdType.MESH
F32 = jnp.float32
BF16 = jnp.bfloat16

SLOT = {0: 0, 7: 1, 1: 2, 6: 3, 2: 4, 5: 5, 3: 6, 4: 7}
DZ = {s: d for d, s in SLOT.items()}


def sem_table():
    names = []
    names += [("y", k) for k in range(1, NY)]
    names += [("sy", k) for k in range(1, NY)]
    names += [("sz", dz, dc) for dz in range(NZ) for dc in range(NC) if (dz, dc) != (0, 0)]
    names += [("az", dz) for dz in range(1, NZ)]
    names += [("ax", dz, dx) for dz in range(NZ) for dx in range(1, NX)]
    names += [("bx", dx) for dx in range(1, NX)]
    names += [("bz", dz, dx) for dz in range(1, NZ) for dx in range(NX)]
    names += [("cc", dz, dx) for dz in range(NZ) for dx in range(NX)]
    names += [("tx", dx, dc) for dx in range(NX) for dc in range(NC) if (dx, dc) != (0, 0)]
    names += [("tz", dz) for dz in range(1, NZ)]
    names += [(kind, sign, q) for kind in ("far", "near", "sum") for sign in (1, -1) for q in range(4)]
    names += [("rz", dz, dc) for dz in range(NZ) for dc in range(NC) if (dz, dc) != (0, 0)]
    return {name: i for i, name in enumerate(names)}


SEMS = sem_table()


def body(h_ref, g_ref, ids_ref, mw_ref, w_ref, out_ref,
         wt, n4, gat, line, sh_src, sh_y, sh_all, lg, st_own, st_x, st_zsrc, st_z,
         fm, fs, pr, far_in, near_in, sum_in, mix, w_sem, loc_sem, ss, rs):
    me = lax.axis_index("expert")
    x = lax.axis_index("tensor")
    y = me // (NZ * NC)
    z = (me // NC) % NZ
    c = me % NC

    def dev(dx=0, dy=0, dz=0, dc=0):
        yy = (y + dy) % NY
        zz = (z + dz) % NZ
        cc = (c + dc) % NC
        return ((yy * NZ + zz) * NC + cc, (x + dx) % NX)

    sent = []

    def send(key, src, dst, to):
        k = SEMS[key]
        copy = pltpu.make_async_remote_copy(
            src_ref=src, dst_ref=dst, send_sem=ss.at[k], recv_sem=rs.at[k],
            device_id=to, device_id_type=MESH)
        copy.start()
        sent.append(copy)

    def arrive(key, dst):
        k = SEMS[key]
        pltpu.make_async_remote_copy(
            src_ref=dst, dst_ref=dst, send_sem=ss.at[k], recv_sem=rs.at[k],
            device_id=dev(dc=1), device_id_type=MESH).wait_recv()

    w_copy = pltpu.make_async_copy(w_ref, wt, w_sem)
    w_copy.start()

    peers = [dev(dy=k) for k in range(1, NY)]
    peers += [dev(dz=1), dev(dz=-1), dev(dx=1), dev(dx=-1), dev(dc=1)]
    barrier = pltpu.get_barrier_semaphore()
    for peer in peers:
        pl.semaphore_signal(barrier, inc=1, device_id=peer, device_id_type=MESH)

    h_all = h_ref[...].astype(F32)
    rms = jnp.sqrt(jnp.mean(h_all * h_all, axis=1, keepdims=True) + EPS)
    cols = pl.ds(pl.multiple_of(x * FQ, FQ), FQ)
    h_q = h_ref[:, cols].astype(F32) / rms
    for e in range(NY):
        n4[e] = (h_q * g_ref[pl.ds(e, 1), cols]).astype(BF16)
    counts = mw_ref[...].astype(F32)
    shares = counts / (counts[0:1] + counts[1:2])
    ids = ids_ref[...]
    line[...] = jnp.zeros_like(line)
    for e in range(NY):
        line[e:e + 1, 0:ROWS_DEV] = jnp.sum(jnp.where(ids == e, shares, 0.0), axis=0, keepdims=True)
    lines = pltpu.roll(line[...], c * 64 + y * ROWS_DEV, 1)
    for e in range(NY):
        sh_src[e] = jnp.broadcast_to(lines[e:e + 1], (8, 128))

    pl.semaphore_wait(barrier, len(peers))

    for k in (2, 1, 3):
        send(("y", k), n4.at[(y + k) % NY], gat.at[0, x, c, y], dev(dy=k))
    for k in (2, 1, 3):
        send(("sy", k), sh_src.at[(y + k) % NY], sh_y.at[k], dev(dy=k))
    own = pltpu.make_async_copy(n4.at[y], gat.at[0, x, c, y], loc_sem)
    own.start()
    own.wait()
    for k in (1, 3, 2):
        arrive(("y", k), gat.at[0, x, c, (y - k) % NY])

    def unit(dz, dx):
        return gat.at[SLOT[dz], (x + dx) % NX, c]

    def part_a(dz, dx):
        return gat.at[SLOT[dz], (x + dx) % NX, c, :, :, pl.ds(0, FA)]

    def part_b(dz, dx):
        return gat.at[SLOT[dz], (x + dx) % NX, c, :, :, pl.ds(FA, FB)]

    def a_along_z(dz, step):
        to = (dz - step) % NZ
        send(("az", to), part_a(dz, 0), part_a(to, 0), dev(dz=step))

    def a_along_x(dz):
        send(("ax", dz, 3), part_a(dz, 0), part_a(dz, 0), dev(dx=1))
        send(("ax", dz, 1), part_a(dz, 0), part_a(dz, 0), dev(dx=-1))

    def a_opposite(dz):
        for dx in (3, 1):
            arrive(("ax", dz, dx), part_a(dz, dx))
            if dx == (3 if dz % 2 == 0 else 1):
                step = 1 if dx == 3 else -1
                send(("ax", dz, 2), part_a(dz, dx), part_a(dz, dx), dev(dx=step))

    def b_along_z(dz, dx, step):
        to = (dz - step) % NZ
        send(("bz", to, dx), part_b(dz, dx), part_b(to, dx), dev(dz=step))

    def to_sibling(dz, dx):
        send(("cc", dz, dx), unit(dz, dx), unit(dz, dx), dev(dc=1))

    def right_hops(dx):
        return 4 if dx in (0, 1) else 3

    def b_round(k, dx):
        if k <= right_hops(dx):
            arrive(("bz", NZ - k, dx), part_b(NZ - k, dx))
            if k < right_hops(dx):
                b_along_z(NZ - k, dx, 1)
        if k <= 7 - right_hops(dx):
            arrive(("bz", k, dx), part_b(k, dx))
            if k < 7 - right_hops(dx):
                b_along_z(k, dx, -1)

    def eye():
        return (lax.broadcasted_iota(jnp.int32, (128, 128), 0)
                == lax.broadcasted_iota(jnp.int32, (128, 128), 1))

    def logits(g, n):
        rows = 2 * 128
        lo, hi = ((0, 512), (512, VD))[n]
        acc = jnp.zeros((rows, hi - lo), F32)
        for xi in range(NX):
            lhs = gat[2 * g:2 * g + 2, xi].reshape(rows, FQ)
            acc += lax.dot_general(
                lhs, wt[lo:hi, xi * FQ:(xi + 1) * FQ],
                (((1,), (1,)), ((), ())), preferred_element_type=F32)
        acc = acc * LOG2E
        if n == 1:
            acc = jnp.concatenate([acc, jnp.full((rows, VP - VD), FAR, F32)], axis=1)
        lg[g * rows:(g + 1) * rows, lo:lo + 512] = acc

    def stats(g):
        rows = 2 * 128
        at = slice(g * rows, (g + 1) * rows)
        lanes = [slice(j * 128, (j + 1) * 128) for j in range(VP // 128)]
        top = lg[at, lanes[0]]
        for ln in lanes[1:]:
            top = jnp.maximum(top, lg[at, ln])
        top = jnp.broadcast_to(jnp.max(top, axis=1, keepdims=True), (rows, 128))
        total = jnp.exp2(lg[at, lanes[0]] - top)
        for ln in lanes[1:]:
            total += jnp.exp2(lg[at, ln] - top)
        total = jnp.broadcast_to(jnp.sum(total, axis=1, keepdims=True), (rows, 128))
        for i in range(2):
            where = (z + DZ[2 * g + i]) % NZ
            for j, col in enumerate((top, total)):
                st_own[pl.ds(j * 8 + where, 1), :] = jnp.sum(
                    jnp.where(eye(), col[i * 128:(i + 1) * 128], 0.0), axis=0, keepdims=True)

    a_along_z(0, 1)
    a_along_z(0, -1)
    send(("bx", 3), part_b(0, 0), part_b(0, 0), dev(dx=1))
    send(("bx", 1), part_b(0, 0), part_b(0, 0), dev(dx=-1))
    a_along_x(0)
    b_along_z(0, 0, 1)
    b_along_z(0, 0, -1)
    to_sibling(0, 0)

    for dx in (3, 1, 2):
        arrive(("bx", dx), part_b(0, dx))
        if dx == 3:
            send(("bx", 2), part_b(0, 3), part_b(0, 3), dev(dx=1))
        b_along_z(0, dx, 1)
        b_along_z(0, dx, -1)

    for k in (1, 3, 2):
        arrive(("sy", k), sh_y.at[k])
    sh_all[0, c] = sh_src[y] + sh_y[1] + sh_y[2] + sh_y[3]

    def finish_x(dz):
        for dx in range(1, NX):
            if dx == 2:
                arrive(("ax", dz, 2), part_a(dz, 2))
            to_sibling(dz, dx)

    def from_sibling(dz):
        for dx in range(NX):
            arrive(("cc", dz, dx), gat.at[SLOT[dz], (x + dx) % NX, 1 - c])

    def a_round(k):
        arrive(("az", NZ - k), part_a(NZ - k, 0))
        if k < 4:
            a_along_z(NZ - k, 1)
        a_along_x(NZ - k)
        if k < 4:
            arrive(("az", k), part_a(k, 0))
            if k < 3:
                a_along_z(k, -1)
            a_along_x(k)

    def b_all(k):
        for dx in range(NX):
            b_round(k, dx)

    def places(k):
        return {0: (0,), 4: (4,)}.get(k, (NZ - k, k))

    def opposite(k):
        for dz in places(k):
            a_opposite(dz)

    def finish(k):
        for dz in places(k):
            if dz:
                to_sibling(dz, 0)
            finish_x(dz)

    a_round(1)
    opposite(0)
    a_round(2)
    b_all(1)
    opposite(1)
    finish(0)
    a_round(3)
    opposite(2)
    b_all(2)
    finish(1)
    a_round(4)
    w_copy.wait()
    from_sibling(0)
    from_sibling(7)
    logits(0, 0)
    opposite(3)
    b_all(3)
    logits(0, 1)
    finish(2)
    opposite(4)
    b_all(4)
    stats(0)
    from_sibling(1)
    from_sibling(6)
    logits(1, 0)
    finish(3)
    finish(4)
    logits(1, 1)
    stats(1)
    from_sibling(2)
    from_sibling(5)
    logits(2, 0)
    logits(2, 1)
    stats(2)
    from_sibling(3)
    from_sibling(4)
    logits(3, 0)
    logits(3, 1)
    stats(3)

    def merge(parts):
        top = parts[0][0]
        for m, _ in parts[1:]:
            top = jnp.maximum(top, m)
        total = jnp.zeros_like(top)
        for m, s in parts:
            total += s * jnp.exp2(m - top)
        return top, total

    near_peers = [(a, b) for a in range(NX) for b in range(NC) if (a, b) != (0, 0)]
    for a, b in near_peers:
        send(("tx", (-a) % NX, b), st_own, st_x.at[(-a) % NX, b], dev(dx=a, dc=b))
    for dz in range(NZ):
        for dc in range(NC):
            if (dz, dc) != (0, 0):
                send(("sz", (-dz) % NZ, dc), sh_all.at[0, c], sh_all.at[(-dz) % NZ, c],
                     dev(dz=dz, dc=dc))
    parts = [(st_own[0:8], st_own[8:16])]
    for a, b in near_peers:
        arrive(("tx", a, b), st_x.at[a, b])
        parts.append((st_x[a, b, 0:8], st_x[a, b, 8:16]))
    top, total = merge(parts)
    st_zsrc[0:8] = top
    st_zsrc[8:16] = total
    for k in range(1, NZ):
        send(("tz", (-k) % NZ), st_zsrc, st_z.at[(-k) % NZ], dev(dz=k))
    parts = [(top, total)]
    for k in range(1, NZ):
        arrive(("tz", k), st_z.at[k])
        parts.append((st_z[k, 0:8], st_z[k, 8:16]))
    top, total = merge(parts)
    fm[...] = top
    fs[...] = total
    for dz in range(NZ):
        for dc in range(NC):
            if (dz, dc) != (0, 0):
                arrive(("sz", dz, dc), sh_all.at[dz, (c + dc) % NC])
    def weigh(s):
        at = (z + DZ[s]) % NZ
        share = sh_all[DZ[s], 0, 0:1] + sh_all[DZ[s], 1, 0:1]
        m_line = fm[pl.ds(at, 1), :]
        f_line = share / fs[pl.ds(at, 1), :]
        m_c = jnp.sum(jnp.where(eye(), m_line, 0.0), axis=1, keepdims=True)
        f_c = jnp.sum(jnp.where(eye(), f_line, 0.0), axis=1, keepdims=True)
        m_c = jnp.broadcast_to(m_c, (128, 128))
        f_c = jnp.broadcast_to(f_c, (128, 128))
        for j in range(VP // 128):
            ln = slice(j * 128, (j + 1) * 128)
            p = (jnp.exp2(lg[s * 128:(s + 1) * 128, ln] - m_c) * f_c).astype(BF16)
            for b in range(NC * NY):
                pr[b % NY, s, b // NY, :, ln] = p[b * ROWS_DEV:(b + 1) * ROWS_DEV]

    ahead, behind, across = (y + 1) % NY, (y + 3) % NY, (y + 2) % NY

    def first_sends(q):
        for s in (q, 4 + q):
            weigh(s)
        send(("far", 1, q), pr.at[across, 4 + q], far_in.at[0, q], dev(dy=1))
        send(("far", -1, q), pr.at[across, q], far_in.at[1, q], dev(dy=-1))
        send(("near", 1, q), pr.at[ahead, q], near_in.at[0, q], dev(dy=1))
        send(("near", -1, q), pr.at[behind, 4 + q], near_in.at[1, q], dev(dy=-1))

    def relay(q):
        for sign, t, s, j in ((1, ahead, 4 + q, 0), (-1, behind, q, 1)):
            arrive(("far", sign, q), far_in.at[j, q])
            pr[t, s] = (pr[t, s].astype(F32) + far_in[j, q].astype(F32)).astype(BF16)
            send(("sum", sign, q), pr.at[t, s], sum_in.at[j, q], dev(dy=sign))

    def combine(q):
        for s, near_j, sum_j in ((q, 0, 1), (4 + q, 1, 0)):
            arrive(("near", 1 - 2 * near_j, q), near_in.at[near_j, q])
            arrive(("sum", 1 - 2 * sum_j, q), sum_in.at[sum_j, q])
            mix[s] = (pr[y, s].astype(F32) + near_in[near_j, q].astype(F32)
                      + sum_in[sum_j, q].astype(F32)).astype(BF16)
            dz = DZ[s]
            for dc in range(NC):
                if (dz, dc) != (0, 0):
                    send(("rz", (-dz) % NZ, dc), mix.at[s, (c + dc) % NC],
                         out_ref.at[z, c], dev(dz=dz, dc=dc))

    first_sends(0)
    first_sends(1)
    for q in range(4):
        relay(q)
        if q < 2:
            first_sends(q + 2)
        if q:
            combine(q - 1)
    combine(3)
    last = pltpu.make_async_copy(mix.at[0, c], out_ref.at[z, c], loc_sem)
    last.start()
    last.wait()
    for dz in range(NZ):
        for dc in range(NC):
            if (dz, dc) != (0, 0):
                arrive(("rz", dz, dc), out_ref.at[(z + dz) % NZ, (c + dc) % NC])
    for copy in sent:
        copy.wait_send()


def spread(mix_ref, out_ref):
    chunks = NZ * NC
    for j in range(chunks):
        start = j * VD
        base, shift = start // 128 * 128, start % 128
        vals = jnp.log(mix_ref[j // NC, j % NC].astype(F32))
        wide = jnp.concatenate([vals, jnp.zeros((ROWS_DEV, 128), F32)], axis=1)
        if shift:
            wide = pltpu.roll(wide, shift, 1)
            lane = lax.broadcasted_iota(jnp.int32, (ROWS_DEV, 128), 1)
            first = jnp.where(lane < shift, out_ref[:, base:base + 128], wide[:, 0:128])
            out_ref[:, base:base + 128] = first
        else:
            out_ref[:, base:base + 128] = wide[:, 0:128]
        end = min(base + wide.shape[1], chunks * VD)
        out_ref[:, base + 128:end] = wide[:, 128:end - base]


def per_device(hidden, norm_gain, head_weight, expert_ids, mix_weight):
    wt_in = jnp.transpose(head_weight.reshape(D, VD))
    vmem = pl.BlockSpec(memory_space=pltpu.VMEM)
    n_sem = len(SEMS)
    returned = pl.pallas_call(
        body,
        out_shape=jax.ShapeDtypeStruct((NZ, NC, ROWS_DEV, VP), BF16),
        in_specs=[vmem, vmem, vmem, vmem, pl.BlockSpec(memory_space=pl.ANY)],
        out_specs=vmem,
        scratch_shapes=[
            pltpu.VMEM((VD, D), BF16),
            pltpu.VMEM((NY, ROWS_DEV, FQ), BF16),
            pltpu.VMEM((NZ, NX, NC, NY, ROWS_DEV, FQ), BF16),
            pltpu.VMEM((8, 128), F32),
            pltpu.VMEM((NY, 8, 128), F32),
            pltpu.VMEM((NY, 8, 128), F32),
            pltpu.VMEM((NZ, NC, 8, 128), F32),
            pltpu.VMEM((NZ * 128, VP), F32),
            pltpu.VMEM((16, 128), F32),
            pltpu.VMEM((NX, NC, 16, 128), F32),
            pltpu.VMEM((16, 128), F32),
            pltpu.VMEM((NZ, 16, 128), F32),
            pltpu.VMEM((8, 128), F32),
            pltpu.VMEM((8, 128), F32),
            pltpu.VMEM((NY, NZ, NC, ROWS_DEV, VP), BF16),
            pltpu.VMEM((2, 4, NC, ROWS_DEV, VP), BF16),
            pltpu.VMEM((2, 4, NC, ROWS_DEV, VP), BF16),
            pltpu.VMEM((2, 4, NC, ROWS_DEV, VP), BF16),
            pltpu.VMEM((NZ, NC, ROWS_DEV, VP), BF16),
            pltpu.SemaphoreType.DMA,
            pltpu.SemaphoreType.DMA,
            pltpu.SemaphoreType.DMA((n_sem,)),
            pltpu.SemaphoreType.DMA((n_sem,)),
        ],
        compiler_params=pltpu.CompilerParams(
            collective_id=0, has_side_effects=True, vmem_limit_bytes=56 * 1024 * 1024),
    )(hidden, norm_gain, expert_ids.T, mix_weight.T, wt_in)
    return pl.pallas_call(
        spread,
        out_shape=jax.ShapeDtypeStruct((ROWS_DEV, NZ * NC * VD), F32),
        in_specs=[vmem],
        out_specs=vmem,
    )(returned)


def solution(mesh):
    placed = (
        P("expert", None),
        P(),
        P(None, "tensor", "expert"),
        P("expert", None),
        P("expert", None),
    )
    return jax.shard_map(
        per_device, mesh=mesh, in_specs=placed, out_specs=P("expert", "tensor"), check_vma=False
    )
```

```python
import jax
import jax.numpy as jnp
from jax import lax
from jax.experimental import pallas as pl
from jax.experimental.pallas import tpu as pltpu
from jax.sharding import PartitionSpec as P

EPS = 1e-05
FAR = -1e30
LOG2E = 1.4426950408889634
NX, NY, NZ, NC = 4, 4, 8, 2
ROWS_DEV = 16
D = 4096
FQ = D // NX
VD = 1002
VP = 1024
FA = 640
FB = FQ - FA
MESH = pl.DeviceIdType.MESH
F32 = jnp.float32
BF16 = jnp.bfloat16

SLOT = {0: 0, 7: 1, 1: 2, 6: 3, 2: 4, 5: 5, 3: 6, 4: 7}
DZ = {s: d for d, s in SLOT.items()}


def sem_table():
    names = []
    names += [("y", k) for k in range(1, NY)]
    names += [("sy", k) for k in range(1, NY)]
    names += [("sz", dz, dc) for dz in range(NZ) for dc in range(NC) if (dz, dc) != (0, 0)]
    names += [("az", dz, k) for dz in range(1, NZ) for k in range(NY)]
    names += [("ax", dz, dx) for dz in range(NZ) for dx in range(1, NX)]
    names += [("bx", dx) for dx in range(1, NX)]
    names += [("bz", dz, dx) for dz in range(1, NZ) for dx in range(NX)]
    names += [("cc", dz, dx) for dz in range(NZ) for dx in range(NX)]
    names += [("tx", dx, dc) for dx in range(NX) for dc in range(NC) if (dx, dc) != (0, 0)]
    names += [("tz", dz) for dz in range(1, NZ)]
    names += [("ye", k, s) for k in range(1, NY) for s in range(NZ)]
    names += [("yf", k) for k in range(1, NY)]
    names += [("rz", dz, dc) for dz in range(NZ) for dc in range(NC) if (dz, dc) != (0, 0)]
    return {name: i for i, name in enumerate(names)}


SEMS = sem_table()


def body(h_ref, g_ref, ids_ref, mw_ref, w_ref, out_ref,
         wt, n4, gat, line, sh_src, sh_y, sh_all, lg, st_own, st_x, st_zsrc, st_z,
         sh_abs, f_own, f_in, pr, y_in, mix, w_sem, loc_sem, ss, rs):
    me = lax.axis_index("expert")
    x = lax.axis_index("tensor")
    y = me // (NZ * NC)
    z = (me // NC) % NZ
    c = me % NC

    def dev(dx=0, dy=0, dz=0, dc=0):
        yy = (y + dy) % NY
        zz = (z + dz) % NZ
        cc = (c + dc) % NC
        return ((yy * NZ + zz) * NC + cc, (x + dx) % NX)

    sent = []

    def send(key, src, dst, to):
        k = SEMS[key]
        copy = pltpu.make_async_remote_copy(
            src_ref=src, dst_ref=dst, send_sem=ss.at[k], recv_sem=rs.at[k],
            device_id=to, device_id_type=MESH)
        copy.start()
        sent.append(copy)

    def arrive(key, dst):
        k = SEMS[key]
        pltpu.make_async_remote_copy(
            src_ref=dst, dst_ref=dst, send_sem=ss.at[k], recv_sem=rs.at[k],
            device_id=dev(dc=1), device_id_type=MESH).wait_recv()

    w_copy = pltpu.make_async_copy(w_ref, wt, w_sem)
    w_copy.start()

    peers = [dev(dy=k) for k in range(1, NY)]
    peers += [dev(dz=1), dev(dz=-1), dev(dx=1), dev(dx=-1), dev(dc=1)]
    barrier = pltpu.get_barrier_semaphore()
    for peer in peers:
        pl.semaphore_signal(barrier, inc=1, device_id=peer, device_id_type=MESH)

    h_all = h_ref[...].astype(F32)
    rms = jnp.sqrt(jnp.mean(h_all * h_all, axis=1, keepdims=True) + EPS)
    cols = pl.ds(pl.multiple_of(x * FQ, FQ), FQ)
    h_q = h_ref[:, cols].astype(F32) / rms
    for e in range(NY):
        n4[e] = (h_q * g_ref[pl.ds(e, 1), cols]).astype(BF16)
    counts = mw_ref[...].astype(F32)
    shares = counts / (counts[0:1] + counts[1:2])
    ids = ids_ref[...]
    line[...] = jnp.zeros_like(line)
    for e in range(NY):
        line[e:e + 1, 0:ROWS_DEV] = jnp.sum(jnp.where(ids == e, shares, 0.0), axis=0, keepdims=True)
    lines = pltpu.roll(line[...], c * 64 + y * ROWS_DEV, 1)
    for e in range(NY):
        sh_src[e] = jnp.broadcast_to(lines[e:e + 1], (8, 128))

    pl.semaphore_wait(barrier, len(peers))

    for k in (2, 1, 3):
        send(("y", k), n4.at[(y + k) % NY], gat.at[0, x, c, y], dev(dy=k))
    for k in (2, 1, 3):
        send(("sy", k), sh_src.at[(y + k) % NY], sh_y.at[k], dev(dy=k))
    def unit(dz, dx):
        return gat.at[SLOT[dz], (x + dx) % NX, c]

    def part_a(dz, dx):
        return gat.at[SLOT[dz], (x + dx) % NX, c, :, :, pl.ds(0, FA)]

    def part_b(dz, dx):
        return gat.at[SLOT[dz], (x + dx) % NX, c, :, :, pl.ds(FA, FB)]

    def piece(dz, k):
        return gat.at[SLOT[dz], x, c, (y - k) % NY, :, pl.ds(0, FA)]

    def a_along_z(dz, k, step):
        to = (dz - step) % NZ
        send(("az", to, k), piece(dz, k), piece(to, k), dev(dz=step))

    def a_along_x(dz):
        send(("ax", dz, 3), part_a(dz, 0), part_a(dz, 0), dev(dx=1))
        send(("ax", dz, 1), part_a(dz, 0), part_a(dz, 0), dev(dx=-1))

    def a_opposite(dz):
        for dx in (3, 1):
            arrive(("ax", dz, dx), part_a(dz, dx))
            if dx == (3 if dz % 2 == 0 else 1):
                step = 1 if dx == 3 else -1
                send(("ax", dz, 2), part_a(dz, dx), part_a(dz, dx), dev(dx=step))

    def b_along_z(dz, dx, step):
        to = (dz - step) % NZ
        send(("bz", to, dx), part_b(dz, dx), part_b(to, dx), dev(dz=step))

    def to_sibling(dz, dx):
        send(("cc", dz, dx), unit(dz, dx), unit(dz, dx), dev(dc=1))

    def right_hops(dx):
        return 4 if dx in (0, 1) else 3

    def b_round(k, dx):
        if k <= right_hops(dx):
            arrive(("bz", NZ - k, dx), part_b(NZ - k, dx))
            if k < right_hops(dx):
                b_along_z(NZ - k, dx, 1)
        if k <= 7 - right_hops(dx):
            arrive(("bz", k, dx), part_b(k, dx))
            if k < 7 - right_hops(dx):
                b_along_z(k, dx, -1)

    def eye():
        return (lax.broadcasted_iota(jnp.int32, (128, 128), 0)
                == lax.broadcasted_iota(jnp.int32, (128, 128), 1))

    def logits(g, n):
        rows = 2 * 128
        lo, hi = ((0, 512), (512, VD))[n]
        acc = jnp.zeros((rows, hi - lo), F32)
        for xi in range(NX):
            lhs = gat[2 * g:2 * g + 2, xi].reshape(rows, FQ)
            acc += lax.dot_general(
                lhs, wt[lo:hi, xi * FQ:(xi + 1) * FQ],
                (((1,), (1,)), ((), ())), preferred_element_type=F32)
        acc = acc * LOG2E
        if n == 1:
            acc = jnp.concatenate([acc, jnp.full((rows, VP - VD), FAR, F32)], axis=1)
        lg[g * rows:(g + 1) * rows, lo:lo + 512] = acc

    def stats(g):
        rows = 2 * 128
        at = slice(g * rows, (g + 1) * rows)
        lanes = [slice(j * 128, (j + 1) * 128) for j in range(VP // 128)]
        top = lg[at, lanes[0]]
        for ln in lanes[1:]:
            top = jnp.maximum(top, lg[at, ln])
        top = jnp.broadcast_to(jnp.max(top, axis=1, keepdims=True), (rows, 128))
        total = jnp.zeros((rows, 128), F32)
        for ln in lanes:
            e = jnp.exp2(lg[at, ln] - top)
            total += e
            low = e.astype(BF16)
            for b in range(2 * NC * NY):
                i, cc, yy = b // (NC * NY), b // NY % NC, b % NY
                pr[yy, 2 * g + i, cc, :, ln] = low[b * ROWS_DEV:(b + 1) * ROWS_DEV]
        for i in range(2):
            for k in (2, 1, 3):
                s = 2 * g + i
                send(("ye", (-k) % NY, s), pr.at[(y + k) % NY, s], y_in.at[(-k) % NY, s], dev(dy=k))
        total = jnp.broadcast_to(jnp.sum(total, axis=1, keepdims=True), (rows, 128))
        for i in range(2):
            where = (z + DZ[2 * g + i]) % NZ
            for j, col in enumerate((top, total)):
                st_own[pl.ds(j * 8 + where, 1), :] = jnp.sum(
                    jnp.where(eye(), col[i * 128:(i + 1) * 128], 0.0), axis=0, keepdims=True)

    gat[0, x, c, y] = n4[y]
    for k in (0, 1, 3, 2):
        if k:
            arrive(("y", k), gat.at[0, x, c, (y - k) % NY])
        a_along_z(0, k, 1)
        a_along_z(0, k, -1)
    send(("bx", 3), part_b(0, 0), part_b(0, 0), dev(dx=1))
    send(("bx", 1), part_b(0, 0), part_b(0, 0), dev(dx=-1))
    a_along_x(0)
    b_along_z(0, 0, 1)
    b_along_z(0, 0, -1)
    to_sibling(0, 0)

    for dx in (3, 1, 2):
        arrive(("bx", dx), part_b(0, dx))
        if dx == 3:
            send(("bx", 2), part_b(0, 3), part_b(0, 3), dev(dx=1))
        b_along_z(0, dx, 1)
        b_along_z(0, dx, -1)

    for k in (1, 3, 2):
        arrive(("sy", k), sh_y.at[k])
    sh_all[0, c] = sh_src[y] + sh_y[1] + sh_y[2] + sh_y[3]

    def finish_x(dz):
        for dx in range(1, NX):
            if dx == 2:
                arrive(("ax", dz, 2), part_a(dz, 2))
            to_sibling(dz, dx)

    def from_sibling(dz):
        for dx in range(NX):
            arrive(("cc", dz, dx), gat.at[SLOT[dz], (x + dx) % NX, 1 - c])

    def a_round(k):
        for p in (0, 1, 3, 2):
            arrive(("az", NZ - k, p), piece(NZ - k, p))
            if k < 4:
                a_along_z(NZ - k, p, 1)
                arrive(("az", k, p), piece(k, p))
                if k < 3:
                    a_along_z(k, p, -1)
        a_along_x(NZ - k)
        if k < 4:
            a_along_x(k)

    def b_all(k):
        for dx in range(NX):
            b_round(k, dx)

    def places(k):
        return {0: (0,), 4: (4,)}.get(k, (NZ - k, k))

    def opposite(k):
        for dz in places(k):
            a_opposite(dz)

    def finish(k):
        for dz in places(k):
            if dz:
                to_sibling(dz, 0)
            finish_x(dz)

    a_round(1)
    opposite(0)
    a_round(2)
    b_all(1)
    opposite(1)
    finish(0)
    a_round(3)
    opposite(2)
    b_all(2)
    finish(1)
    a_round(4)
    w_copy.wait()
    from_sibling(0)
    from_sibling(7)
    logits(0, 0)
    opposite(3)
    b_all(3)
    logits(0, 1)
    finish(2)
    opposite(4)
    b_all(4)
    stats(0)
    from_sibling(1)
    from_sibling(6)
    logits(1, 0)
    finish(3)
    finish(4)
    logits(1, 1)
    stats(1)
    from_sibling(2)
    from_sibling(5)
    logits(2, 0)
    logits(2, 1)
    stats(2)
    from_sibling(3)
    from_sibling(4)
    for dz in range(NZ):
        for dc in range(NC):
            if (dz, dc) != (0, 0):
                send(("sz", (-dz) % NZ, dc), sh_all.at[0, c], sh_all.at[(-dz) % NZ, c],
                     dev(dz=dz, dc=dc))
    logits(3, 0)
    logits(3, 1)
    stats(3)

    def merge(parts):
        top = parts[0][0]
        for m, _ in parts[1:]:
            top = jnp.maximum(top, m)
        total = jnp.zeros_like(top)
        for m, s in parts:
            total += s * jnp.exp2(m - top)
        return top, total

    near_peers = [(a, b) for a in range(NX) for b in range(NC) if (a, b) != (0, 0)]
    for a, b in near_peers:
        send(("tx", (-a) % NX, b), st_own, st_x.at[(-a) % NX, b], dev(dx=a, dc=b))
    parts = [(st_own[0:8], st_own[8:16])]
    for a, b in near_peers:
        arrive(("tx", a, b), st_x.at[a, b])
        parts.append((st_x[a, b, 0:8], st_x[a, b, 8:16]))
    top, total = merge(parts)
    st_zsrc[0:8] = top
    st_zsrc[8:16] = total
    for k in range(1, NZ):
        send(("tz", (-k) % NZ), st_zsrc, st_z.at[(-k) % NZ], dev(dz=k))
    parts = [(top, total)]
    for k in range(1, NZ):
        arrive(("tz", k), st_z.at[k])
        parts.append((st_z[k, 0:8], st_z[k, 8:16]))
    top, total = merge(parts)
    for dz in range(NZ):
        for dc in range(NC):
            if (dz, dc) != (0, 0):
                arrive(("sz", dz, dc), sh_all.at[dz, (c + dc) % NC])
        sh_abs[pl.ds((z + dz) % NZ, 1), :] = sh_all[dz, 0, 0:1] + sh_all[dz, 1, 0:1]
    f_own[...] = sh_abs[...] * jnp.exp2(st_own[0:8] - top) / total
    for k in (2, 1, 3):
        send(("yf", (-k) % NY), f_own, f_in.at[(-k) % NY], dev(dy=k))
    for k in range(1, NY):
        arrive(("yf", k), f_in.at[k])

    lane = lax.broadcasted_iota(jnp.int32, (NC * ROWS_DEV, 128), 1)
    row = lax.broadcasted_iota(jnp.int32, (NC * ROWS_DEV, 128), 0)
    take = lane == row // ROWS_DEV * 64 + y * ROWS_DEV + row % ROWS_DEV

    def mixing(s):
        dz = DZ[s]
        at = pl.ds((z + dz) % NZ, 1)
        for k in range(1, NY):
            arrive(("ye", k, s), y_in.at[k, s])
        cols = []
        for k in range(NY):
            factors = f_in[k, at, :] if k else f_own[at, :]
            col = jnp.sum(jnp.where(take, factors, 0.0), axis=1, keepdims=True)
            cols.append(jnp.broadcast_to(col, (NC * ROWS_DEV, 128)))
        for j in range(VP // 128):
            ln = slice(j * 128, (j + 1) * 128)
            mixed = pr[y, s, :, :, ln].reshape(NC * ROWS_DEV, 128).astype(F32) * cols[0]
            for k in range(1, NY):
                mixed += y_in[k, s, :, :, ln].reshape(NC * ROWS_DEV, 128).astype(F32) * cols[k]
            mix[s, :, :, ln] = mixed.astype(BF16).reshape(NC, ROWS_DEV, 128)
        for dc in range(NC):
            if (dz, dc) != (0, 0):
                send(("rz", (-dz) % NZ, dc), mix.at[s, (c + dc) % NC],
                     out_ref.at[z, c], dev(dz=dz, dc=dc))

    for dz in (4, 3, 5, 2, 6, 1, 7, 0):
        mixing(SLOT[dz])
    last = pltpu.make_async_copy(mix.at[0, c], out_ref.at[z, c], loc_sem)
    last.start()
    last.wait()
    for dz in range(NZ):
        for dc in range(NC):
            if (dz, dc) != (0, 0):
                arrive(("rz", dz, dc), out_ref.at[(z + dz) % NZ, (c + dc) % NC])
    for copy in sent:
        copy.wait_send()


def spread(mix_ref, out_ref):
    chunks = NZ * NC
    for j in range(chunks):
        start = j * VD
        base, shift = start // 128 * 128, start % 128
        vals = jnp.log(mix_ref[j // NC, j % NC].astype(F32))
        wide = jnp.concatenate([vals, jnp.zeros((ROWS_DEV, 128), F32)], axis=1)
        if shift:
            wide = pltpu.roll(wide, shift, 1)
            lane = lax.broadcasted_iota(jnp.int32, (ROWS_DEV, 128), 1)
            first = jnp.where(lane < shift, out_ref[:, base:base + 128], wide[:, 0:128])
            out_ref[:, base:base + 128] = first
        else:
            out_ref[:, base:base + 128] = wide[:, 0:128]
        end = min(base + wide.shape[1], chunks * VD)
        out_ref[:, base + 128:end] = wide[:, 128:end - base]


def per_device(hidden, norm_gain, head_weight, expert_ids, mix_weight):
    wt_in = jnp.transpose(head_weight.reshape(D, VD))
    vmem = pl.BlockSpec(memory_space=pltpu.VMEM)
    n_sem = len(SEMS)
    returned = pl.pallas_call(
        body,
        out_shape=jax.ShapeDtypeStruct((NZ, NC, ROWS_DEV, VP), BF16),
        in_specs=[vmem, vmem, vmem, vmem, pl.BlockSpec(memory_space=pl.ANY)],
        out_specs=vmem,
        scratch_shapes=[
            pltpu.VMEM((VD, D), BF16),
            pltpu.VMEM((NY, ROWS_DEV, FQ), BF16),
            pltpu.VMEM((NZ, NX, NC, NY, ROWS_DEV, FQ), BF16),
            pltpu.VMEM((8, 128), F32),
            pltpu.VMEM((NY, 8, 128), F32),
            pltpu.VMEM((NY, 8, 128), F32),
            pltpu.VMEM((NZ, NC, 8, 128), F32),
            pltpu.VMEM((NZ * 128, VP), F32),
            pltpu.VMEM((16, 128), F32),
            pltpu.VMEM((NX, NC, 16, 128), F32),
            pltpu.VMEM((16, 128), F32),
            pltpu.VMEM((NZ, 16, 128), F32),
            pltpu.VMEM((8, 128), F32),
            pltpu.VMEM((8, 128), F32),
            pltpu.VMEM((NY, 8, 128), F32),
            pltpu.VMEM((NY, NZ, NC, ROWS_DEV, VP), BF16),
            pltpu.VMEM((NY, NZ, NC, ROWS_DEV, VP), BF16),
            pltpu.VMEM((NZ, NC, ROWS_DEV, VP), BF16),
            pltpu.SemaphoreType.DMA,
            pltpu.SemaphoreType.DMA,
            pltpu.SemaphoreType.DMA((n_sem,)),
            pltpu.SemaphoreType.DMA((n_sem,)),
        ],
        compiler_params=pltpu.CompilerParams(
            collective_id=0, has_side_effects=True, vmem_limit_bytes=56 * 1024 * 1024),
    )(hidden, norm_gain, expert_ids.T, mix_weight.T, wt_in)
    return pl.pallas_call(
        spread,
        out_shape=jax.ShapeDtypeStruct((ROWS_DEV, NZ * NC * VD), F32),
        in_specs=[vmem],
        out_specs=vmem,
    )(returned)


def solution(mesh):
    placed = (
        P("expert", None),
        P(),
        P(None, "tensor", "expert"),
        P("expert", None),
        P("expert", None),
    )
    return jax.shard_map(
        per_device, mesh=mesh, in_specs=placed, out_specs=P("expert", "tensor"), check_vma=False
    )
```

```python
import jax
import jax.numpy as jnp
from jax import lax
from jax.experimental import pallas as pl
from jax.experimental.pallas import tpu as pltpu
from jax.sharding import PartitionSpec as P

EPS = 1e-05
FAR = -1e30
LOG2E = 1.4426950408889634
NX, NY, NZ, NC = 4, 4, 8, 2
ROWS_DEV = 16
D = 4096
FQ = D // NX
VD = 1002
VP = 1024
FA = 640
FB = FQ - FA
MESH = pl.DeviceIdType.MESH
F32 = jnp.float32
BF16 = jnp.bfloat16

SLOT = {0: 0, 7: 1, 1: 2, 6: 3, 2: 4, 5: 5, 3: 6, 4: 7}
DZ = {s: d for d, s in SLOT.items()}


def sem_table():
    names = []
    names += [("y", k) for k in range(1, NY)]
    names += [("sy", k) for k in range(1, NY)]
    names += [("sz", dz, dc) for dz in range(NZ) for dc in range(NC) if (dz, dc) != (0, 0)]
    names += [("az", dz, k) for dz in range(1, NZ) for k in range(NY)]
    names += [("ax", dz, dx) for dz in range(NZ) for dx in range(1, NX)]
    names += [("bx", dx) for dx in range(1, NX)]
    names += [("bz", dz, dx) for dz in range(1, NZ) for dx in range(NX)]
    names += [("cc", dz, dx) for dz in range(NZ) for dx in range(NX)]
    names += [("tx", dx, dc) for dx in range(NX) for dc in range(NC) if (dx, dc) != (0, 0)]
    names += [("tz", dz) for dz in range(1, NZ)]
    names += [("ye", k, s) for k in range(1, NY) for s in range(NZ)]
    names += [("yf", k) for k in range(1, NY)]
    names += [("rz", dz, dc) for dz in range(NZ) for dc in range(NC) if (dz, dc) != (0, 0)]
    return {name: i for i, name in enumerate(names)}


SEMS = sem_table()


def body(h_ref, g_ref, ids_ref, mw_ref, w_ref, out_ref,
         wt, n4, gat, line, sh_src, sh_y, sh_all, lg, st_own, st_x, st_zsrc, st_z,
         sh_abs, f_own, f_in, pr, y_in, mix, w_sem, loc_sem, ss, rs):
    me = lax.axis_index("expert")
    x = lax.axis_index("tensor")
    y = me // (NZ * NC)
    z = (me // NC) % NZ
    c = me % NC

    def dev(dx=0, dy=0, dz=0, dc=0):
        yy = (y + dy) % NY
        zz = (z + dz) % NZ
        cc = (c + dc) % NC
        return ((yy * NZ + zz) * NC + cc, (x + dx) % NX)

    sent = []

    def send(key, src, dst, to):
        k = SEMS[key]
        copy = pltpu.make_async_remote_copy(
            src_ref=src, dst_ref=dst, send_sem=ss.at[k], recv_sem=rs.at[k],
            device_id=to, device_id_type=MESH)
        copy.start()
        sent.append(copy)

    def arrive(key, dst):
        k = SEMS[key]
        pltpu.make_async_remote_copy(
            src_ref=dst, dst_ref=dst, send_sem=ss.at[k], recv_sem=rs.at[k],
            device_id=dev(dc=1), device_id_type=MESH).wait_recv()

    w_copy = pltpu.make_async_copy(w_ref, wt, w_sem)
    w_copy.start()

    peers = [dev(dy=k) for k in range(1, NY)]
    peers += [dev(dz=1), dev(dz=-1), dev(dx=1), dev(dx=2), dev(dx=-1), dev(dc=1)]
    barrier = pltpu.get_barrier_semaphore()
    for peer in peers:
        pl.semaphore_signal(barrier, inc=1, device_id=peer, device_id_type=MESH)

    h_all = h_ref[...].astype(F32)
    rms = jnp.sqrt(jnp.mean(h_all * h_all, axis=1, keepdims=True) + EPS)
    cols = pl.ds(pl.multiple_of(x * FQ, FQ), FQ)
    h_q = h_ref[:, cols].astype(F32) / rms
    for e in range(NY):
        n4[e] = (h_q * g_ref[pl.ds(e, 1), cols]).astype(BF16)
    counts = mw_ref[...].astype(F32)
    shares = counts / (counts[0:1] + counts[1:2])
    ids = ids_ref[...]
    line[...] = jnp.zeros_like(line)
    for e in range(NY):
        line[e:e + 1, 0:ROWS_DEV] = jnp.sum(jnp.where(ids == e, shares, 0.0), axis=0, keepdims=True)
    lines = pltpu.roll(line[...], c * 64 + y * ROWS_DEV, 1)
    for e in range(NY):
        sh_src[e] = jnp.broadcast_to(lines[e:e + 1], (8, 128))

    pl.semaphore_wait(barrier, len(peers))

    for k in (2, 1, 3):
        send(("y", k), n4.at[(y + k) % NY], gat.at[0, x, c, y], dev(dy=k))
    for k in (2, 1, 3):
        send(("sy", k), sh_src.at[(y + k) % NY], sh_y.at[k], dev(dy=k))
    def unit(dz, dx):
        return gat.at[SLOT[dz], (x + dx) % NX, c]

    def part_a(dz, dx):
        return gat.at[SLOT[dz], (x + dx) % NX, c, :, :, pl.ds(0, FA)]

    def part_b(dz, dx):
        return gat.at[SLOT[dz], (x + dx) % NX, c, :, :, pl.ds(FA, FB)]

    def piece(dz, k):
        return gat.at[SLOT[dz], x, c, (y - k) % NY, :, pl.ds(0, FA)]

    def a_along_z(dz, k, step):
        to = (dz - step) % NZ
        send(("az", to, k), piece(dz, k), piece(to, k), dev(dz=step))

    def a_along_x(dz):
        send(("ax", dz, 3), part_a(dz, 0), part_a(dz, 0), dev(dx=1))
        send(("ax", dz, 1), part_a(dz, 0), part_a(dz, 0), dev(dx=-1))

    def a_opposite(dz):
        for dx in (3, 1):
            arrive(("ax", dz, dx), part_a(dz, dx))
            if dx == (3 if dz % 2 == 0 else 1):
                step = 1 if dx == 3 else -1
                send(("ax", dz, 2), part_a(dz, dx), part_a(dz, dx), dev(dx=step))

    def b_along_z(dz, dx, step):
        to = (dz - step) % NZ
        send(("bz", to, dx), part_b(dz, dx), part_b(to, dx), dev(dz=step))

    def to_sibling(dz, dx):
        send(("cc", dz, dx), unit(dz, dx), unit(dz, dx), dev(dc=1))

    def right_hops(dx):
        return 4 if dx in (0, 1) else 3

    def b_round(k, dx):
        if k <= right_hops(dx):
            arrive(("bz", NZ - k, dx), part_b(NZ - k, dx))
            if k < right_hops(dx):
                b_along_z(NZ - k, dx, 1)
        if k <= 7 - right_hops(dx):
            arrive(("bz", k, dx), part_b(k, dx))
            if k < 7 - right_hops(dx):
                b_along_z(k, dx, -1)

    def eye():
        return (lax.broadcasted_iota(jnp.int32, (128, 128), 0)
                == lax.broadcasted_iota(jnp.int32, (128, 128), 1))

    def logits(g, n):
        rows = 2 * 128
        lo, hi = ((0, 512), (512, VD))[n]
        acc = jnp.zeros((rows, hi - lo), F32)
        for xi in range(NX):
            lhs = gat[2 * g:2 * g + 2, xi].reshape(rows, FQ)
            acc += lax.dot_general(
                lhs, wt[lo:hi, xi * FQ:(xi + 1) * FQ],
                (((1,), (1,)), ((), ())), preferred_element_type=F32)
        acc = acc * LOG2E
        if n == 1:
            acc = jnp.concatenate([acc, jnp.full((rows, VP - VD), FAR, F32)], axis=1)
        lg[g * rows:(g + 1) * rows, lo:lo + 512] = acc

    def stats(g):
        rows = 2 * 128
        at = slice(g * rows, (g + 1) * rows)
        lanes = [slice(j * 128, (j + 1) * 128) for j in range(VP // 128)]
        top = lg[at, lanes[0]]
        for ln in lanes[1:]:
            top = jnp.maximum(top, lg[at, ln])
        top = jnp.broadcast_to(jnp.max(top, axis=1, keepdims=True), (rows, 128))
        total = jnp.zeros((rows, 128), F32)
        for ln in lanes:
            e = jnp.exp2(lg[at, ln] - top)
            total += e
            low = e.astype(BF16)
            for b in range(2 * NC * NY):
                i, cc, yy = b // (NC * NY), b // NY % NC, b % NY
                pr[yy, 2 * g + i, cc, :, ln] = low[b * ROWS_DEV:(b + 1) * ROWS_DEV]
        for i in range(2):
            for k in (2, 1, 3):
                s = 2 * g + i
                send(("ye", (-k) % NY, s), pr.at[(y + k) % NY, s], y_in.at[(-k) % NY, s], dev(dy=k))
        total = jnp.broadcast_to(jnp.sum(total, axis=1, keepdims=True), (rows, 128))
        for i in range(2):
            where = (z + DZ[2 * g + i]) % NZ
            for j, col in enumerate((top, total)):
                st_own[pl.ds(j * 8 + where, 1), :] = jnp.sum(
                    jnp.where(eye(), col[i * 128:(i + 1) * 128], 0.0), axis=0, keepdims=True)

    gat[0, x, c, y] = n4[y]
    for k in (0, 1, 3, 2):
        if k:
            arrive(("y", k), gat.at[0, x, c, (y - k) % NY])
        a_along_z(0, k, 1)
        a_along_z(0, k, -1)
    send(("bx", 2), part_b(0, 0), part_b(0, 0), dev(dx=2))
    send(("bx", 3), part_b(0, 0), part_b(0, 0), dev(dx=1))
    send(("bx", 1), part_b(0, 0), part_b(0, 0), dev(dx=-1))
    a_along_x(0)
    b_along_z(0, 0, 1)
    b_along_z(0, 0, -1)
    to_sibling(0, 0)

    for dx in (3, 1, 2):
        arrive(("bx", dx), part_b(0, dx))
        b_along_z(0, dx, 1)
        b_along_z(0, dx, -1)

    for k in (1, 3, 2):
        arrive(("sy", k), sh_y.at[k])
    sh_all[0, c] = sh_src[y] + sh_y[1] + sh_y[2] + sh_y[3]

    def finish_x(dz):
        for dx in range(1, NX):
            if dx == 2:
                arrive(("ax", dz, 2), part_a(dz, 2))
            to_sibling(dz, dx)

    def from_sibling(dz):
        for dx in range(NX):
            arrive(("cc", dz, dx), gat.at[SLOT[dz], (x + dx) % NX, 1 - c])

    def a_round(k):
        for p in (0, 1, 3, 2):
            arrive(("az", NZ - k, p), piece(NZ - k, p))
            if k < 4:
                a_along_z(NZ - k, p, 1)
                arrive(("az", k, p), piece(k, p))
                if k < 3:
                    a_along_z(k, p, -1)
        a_along_x(NZ - k)
        if k < 4:
            a_along_x(k)

    def b_all(k):
        for dx in range(NX):
            b_round(k, dx)

    def places(k):
        return {0: (0,), 4: (4,)}.get(k, (NZ - k, k))

    def opposite(k):
        for dz in places(k):
            a_opposite(dz)

    def finish(k):
        for dz in places(k):
            if dz:
                to_sibling(dz, 0)
            finish_x(dz)

    def shares_out():
        for dz in range(NZ):
            for dc in range(NC):
                if (dz, dc) != (0, 0):
                    send(("sz", (-dz) % NZ, dc), sh_all.at[0, c], sh_all.at[(-dz) % NZ, c],
                         dev(dz=dz, dc=dc))

    a_round(1)
    opposite(0)
    a_round(2)
    b_all(1)
    opposite(1)
    finish(0)
    a_round(3)
    opposite(2)
    b_all(2)
    finish(1)
    a_round(4)
    w_copy.wait()
    from_sibling(0)
    from_sibling(7)
    logits(0, 0)
    opposite(3)
    b_all(3)
    logits(0, 1)
    finish(2)
    stats(0)
    opposite(4)
    b_all(4)
    from_sibling(1)
    from_sibling(6)
    logits(1, 0)
    finish(3)
    finish(4)
    logits(1, 1)
    stats(1)
    from_sibling(2)
    from_sibling(5)
    logits(2, 0)
    logits(2, 1)
    stats(2)
    from_sibling(3)
    from_sibling(4)
    shares_out()
    logits(3, 0)
    logits(3, 1)
    stats(3)

    def merge(parts):
        top = parts[0][0]
        for m, _ in parts[1:]:
            top = jnp.maximum(top, m)
        total = jnp.zeros_like(top)
        for m, s in parts:
            total += s * jnp.exp2(m - top)
        return top, total

    near_peers = [(a, b) for a in range(NX) for b in range(NC) if (a, b) != (0, 0)]
    for a, b in near_peers:
        send(("tx", (-a) % NX, b), st_own, st_x.at[(-a) % NX, b], dev(dx=a, dc=b))
    parts = [(st_own[0:8], st_own[8:16])]
    for a, b in near_peers:
        arrive(("tx", a, b), st_x.at[a, b])
        parts.append((st_x[a, b, 0:8], st_x[a, b, 8:16]))
    top, total = merge(parts)
    st_zsrc[0:8] = top
    st_zsrc[8:16] = total
    for k in range(1, NZ):
        send(("tz", (-k) % NZ), st_zsrc, st_z.at[(-k) % NZ], dev(dz=k))
    parts = [(top, total)]
    for k in range(1, NZ):
        arrive(("tz", k), st_z.at[k])
        parts.append((st_z[k, 0:8], st_z[k, 8:16]))
    top, total = merge(parts)
    for dz in range(NZ):
        for dc in range(NC):
            if (dz, dc) != (0, 0):
                arrive(("sz", dz, dc), sh_all.at[dz, (c + dc) % NC])
        sh_abs[pl.ds((z + dz) % NZ, 1), :] = sh_all[dz, 0, 0:1] + sh_all[dz, 1, 0:1]
    f_own[...] = sh_abs[...] * jnp.exp2(st_own[0:8] - top) / total
    for k in (2, 1, 3):
        send(("yf", (-k) % NY), f_own, f_in.at[(-k) % NY], dev(dy=k))
    for k in range(1, NY):
        arrive(("yf", k), f_in.at[k])

    lane = lax.broadcasted_iota(jnp.int32, (NC * ROWS_DEV, 128), 1)
    row = lax.broadcasted_iota(jnp.int32, (NC * ROWS_DEV, 128), 0)
    take = lane == row // ROWS_DEV * 64 + y * ROWS_DEV + row % ROWS_DEV

    def mixing(s):
        dz = DZ[s]
        at = pl.ds((z + dz) % NZ, 1)
        for k in range(1, NY):
            arrive(("ye", k, s), y_in.at[k, s])
        cols = []
        for k in range(NY):
            factors = f_in[k, at, :] if k else f_own[at, :]
            col = jnp.sum(jnp.where(take, factors, 0.0), axis=1, keepdims=True)
            cols.append(jnp.broadcast_to(col, (NC * ROWS_DEV, 128)))
        for j in range(VP // 128):
            ln = slice(j * 128, (j + 1) * 128)
            mixed = pr[y, s, :, :, ln].reshape(NC * ROWS_DEV, 128).astype(F32) * cols[0]
            for k in range(1, NY):
                mixed += y_in[k, s, :, :, ln].reshape(NC * ROWS_DEV, 128).astype(F32) * cols[k]
            mix[s, :, :, ln] = mixed.astype(BF16).reshape(NC, ROWS_DEV, 128)
        for dc in range(NC):
            if (dz, dc) != (0, 0):
                send(("rz", (-dz) % NZ, dc), mix.at[s, (c + dc) % NC],
                     out_ref.at[z, c], dev(dz=dz, dc=dc))

    for dz in (4, 3, 5, 2, 6, 1, 7, 0):
        mixing(SLOT[dz])
    last = pltpu.make_async_copy(mix.at[0, c], out_ref.at[z, c], loc_sem)
    last.start()
    last.wait()
    for dz in range(NZ):
        for dc in range(NC):
            if (dz, dc) != (0, 0):
                arrive(("rz", dz, dc), out_ref.at[(z + dz) % NZ, (c + dc) % NC])
    for copy in sent:
        copy.wait_send()


def spread(mix_ref, out_ref):
    chunks = NZ * NC
    for j in range(chunks):
        start = j * VD
        base, shift = start // 128 * 128, start % 128
        vals = jnp.log(mix_ref[j // NC, j % NC].astype(F32))
        wide = jnp.concatenate([vals, jnp.zeros((ROWS_DEV, 128), F32)], axis=1)
        if shift:
            wide = pltpu.roll(wide, shift, 1)
            lane = lax.broadcasted_iota(jnp.int32, (ROWS_DEV, 128), 1)
            first = jnp.where(lane < shift, out_ref[:, base:base + 128], wide[:, 0:128])
            out_ref[:, base:base + 128] = first
        else:
            out_ref[:, base:base + 128] = wide[:, 0:128]
        end = min(base + wide.shape[1], chunks * VD)
        out_ref[:, base + 128:end] = wide[:, 128:end - base]


def per_device(hidden, norm_gain, head_weight, expert_ids, mix_weight):
    wt_in = jnp.transpose(head_weight.reshape(D, VD))
    vmem = pl.BlockSpec(memory_space=pltpu.VMEM)
    n_sem = len(SEMS)
    returned = pl.pallas_call(
        body,
        out_shape=jax.ShapeDtypeStruct((NZ, NC, ROWS_DEV, VP), BF16),
        in_specs=[vmem, vmem, vmem, vmem, pl.BlockSpec(memory_space=pl.ANY)],
        out_specs=vmem,
        scratch_shapes=[
            pltpu.VMEM((VD, D), BF16),
            pltpu.VMEM((NY, ROWS_DEV, FQ), BF16),
            pltpu.VMEM((NZ, NX, NC, NY, ROWS_DEV, FQ), BF16),
            pltpu.VMEM((8, 128), F32),
            pltpu.VMEM((NY, 8, 128), F32),
            pltpu.VMEM((NY, 8, 128), F32),
            pltpu.VMEM((NZ, NC, 8, 128), F32),
            pltpu.VMEM((NZ * 128, VP), F32),
            pltpu.VMEM((16, 128), F32),
            pltpu.VMEM((NX, NC, 16, 128), F32),
            pltpu.VMEM((16, 128), F32),
            pltpu.VMEM((NZ, 16, 128), F32),
            pltpu.VMEM((8, 128), F32),
            pltpu.VMEM((8, 128), F32),
            pltpu.VMEM((NY, 8, 128), F32),
            pltpu.VMEM((NY, NZ, NC, ROWS_DEV, VP), BF16),
            pltpu.VMEM((NY, NZ, NC, ROWS_DEV, VP), BF16),
            pltpu.VMEM((NZ, NC, ROWS_DEV, VP), BF16),
            pltpu.SemaphoreType.DMA,
            pltpu.SemaphoreType.DMA,
            pltpu.SemaphoreType.DMA((n_sem,)),
            pltpu.SemaphoreType.DMA((n_sem,)),
        ],
        compiler_params=pltpu.CompilerParams(
            collective_id=0, has_side_effects=True, vmem_limit_bytes=56 * 1024 * 1024),
    )(hidden, norm_gain, expert_ids.T, mix_weight.T, wt_in)
    return pl.pallas_call(
        spread,
        out_shape=jax.ShapeDtypeStruct((ROWS_DEV, NZ * NC * VD), F32),
        in_specs=[vmem],
        out_specs=vmem,
    )(returned)


def solution(mesh):
    placed = (
        P("expert", None),
        P(),
        P(None, "tensor", "expert"),
        P("expert", None),
        P("expert", None),
    )
    return jax.shard_map(
        per_device, mesh=mesh, in_specs=placed, out_specs=P("expert", "tensor"), check_vma=False
    )
```

```python
import jax
import jax.numpy as jnp
from jax import lax
from jax.experimental import pallas as pl
from jax.experimental.pallas import tpu as pltpu
from jax.sharding import PartitionSpec as P

EPS = 1e-05
FAR = -1e30
LOG2E = 1.4426950408889634
NX, NY, NZ, NC = 4, 4, 8, 2
ROWS_DEV = 16
D = 4096
FQ = D // NX
VD = 1002
VP = 1024
FA = 640
FB = FQ - FA
MESH = pl.DeviceIdType.MESH
F32 = jnp.float32
BF16 = jnp.bfloat16

SLOT = {0: 0, 7: 1, 1: 2, 6: 3, 2: 4, 5: 5, 3: 6, 4: 7}
DZ = {s: d for d, s in SLOT.items()}


def sem_table():
    names = []
    names += [("y", k) for k in range(1, NY)]
    names += [("sy", k) for k in range(1, NY)]
    names += [("sz", dz, dc) for dz in range(NZ) for dc in range(NC) if (dz, dc) != (0, 0)]
    names += [("az", dz, k) for dz in range(1, NZ) for k in range(NY)]
    names += [("ax", dz, dx) for dz in range(NZ) for dx in range(1, NX)]
    names += [("bx", dx) for dx in range(1, NX)]
    names += [("bz", dz, dx) for dz in range(1, NZ) for dx in range(NX)]
    names += [("cc", dz, dx) for dz in range(NZ) for dx in range(NX)]
    names += [("tx", dx, dc) for dx in range(NX) for dc in range(NC) if (dx, dc) != (0, 0)]
    names += [("tz", dz) for dz in range(1, NZ)]
    names += [("ye", k, s) for k in range(1, NY) for s in range(NZ)]
    names += [("yf", k) for k in range(1, NY)]
    names += [("rz", dz, dc) for dz in range(NZ) for dc in range(NC) if (dz, dc) != (0, 0)]
    return {name: i for i, name in enumerate(names)}


SEMS = sem_table()


def body(h_ref, g_ref, ids_ref, mw_ref, w_ref, out_ref,
         wt, n4, gat, line, sh_src, sh_y, sh_all, lg, st_own, st_x, st_zsrc, st_z,
         sh_abs, f_own, f_in, pr, y_in, mix, w_sem, loc_sem, ss, rs):
    me = lax.axis_index("expert")
    x = lax.axis_index("tensor")
    y = me // (NZ * NC)
    z = (me // NC) % NZ
    c = me % NC

    def dev(dx=0, dy=0, dz=0, dc=0):
        yy = (y + dy) % NY
        zz = (z + dz) % NZ
        cc = (c + dc) % NC
        return ((yy * NZ + zz) * NC + cc, (x + dx) % NX)

    sent = []

    def send(key, src, dst, to):
        k = SEMS[key]
        copy = pltpu.make_async_remote_copy(
            src_ref=src, dst_ref=dst, send_sem=ss.at[k], recv_sem=rs.at[k],
            device_id=to, device_id_type=MESH)
        copy.start()
        sent.append(copy)

    def arrive(key, dst):
        k = SEMS[key]
        pltpu.make_async_remote_copy(
            src_ref=dst, dst_ref=dst, send_sem=ss.at[k], recv_sem=rs.at[k],
            device_id=dev(dc=1), device_id_type=MESH).wait_recv()

    w_copy = pltpu.make_async_copy(w_ref, wt, w_sem)
    w_copy.start()

    peers = [dev(dy=k) for k in range(1, NY)]
    peers += [dev(dz=1), dev(dz=-1), dev(dx=1), dev(dx=2), dev(dx=-1), dev(dc=1)]
    barrier = pltpu.get_barrier_semaphore()
    for peer in peers:
        pl.semaphore_signal(barrier, inc=1, device_id=peer, device_id_type=MESH)

    h_all = h_ref[...].astype(F32)
    rms = jnp.sqrt(jnp.mean(h_all * h_all, axis=1, keepdims=True) + EPS)
    cols = pl.ds(pl.multiple_of(x * FQ, FQ), FQ)
    h_q = h_ref[:, cols].astype(F32) / rms
    for e in range(NY):
        n4[e] = (h_q * g_ref[pl.ds(e, 1), cols]).astype(BF16)
    counts = mw_ref[...].astype(F32)
    shares = counts / (counts[0:1] + counts[1:2])
    ids = ids_ref[...]
    line[...] = jnp.zeros_like(line)
    for e in range(NY):
        line[e:e + 1, 0:ROWS_DEV] = jnp.sum(jnp.where(ids == e, shares, 0.0), axis=0, keepdims=True)
    lines = pltpu.roll(line[...], c * 64 + y * ROWS_DEV, 1)
    for e in range(NY):
        sh_src[e] = jnp.broadcast_to(lines[e:e + 1], (8, 128))

    pl.semaphore_wait(barrier, len(peers))

    for k in (2, 1, 3):
        send(("y", k), n4.at[(y + k) % NY], gat.at[0, x, c, y], dev(dy=k))
    for k in (2, 1, 3):
        send(("sy", k), sh_src.at[(y + k) % NY], sh_y.at[k], dev(dy=k))
    def unit(dz, dx):
        return gat.at[SLOT[dz], (x + dx) % NX, c]

    def part_a(dz, dx):
        return gat.at[SLOT[dz], (x + dx) % NX, c, :, :, pl.ds(0, FA)]

    def part_b(dz, dx):
        return gat.at[SLOT[dz], (x + dx) % NX, c, :, :, pl.ds(FA, FB)]

    def piece(dz, k):
        return gat.at[SLOT[dz], x, c, (y - k) % NY, :, pl.ds(0, FA)]

    def a_along_z(dz, k, step):
        to = (dz - step) % NZ
        send(("az", to, k), piece(dz, k), piece(to, k), dev(dz=step))

    def a_along_x(dz):
        send(("ax", dz, 3), part_a(dz, 0), part_a(dz, 0), dev(dx=1))
        send(("ax", dz, 1), part_a(dz, 0), part_a(dz, 0), dev(dx=-1))

    def a_opposite(dz):
        for dx in (3, 1):
            arrive(("ax", dz, dx), part_a(dz, dx))
            if dx == (3 if dz % 2 == 0 else 1):
                step = 1 if dx == 3 else -1
                send(("ax", dz, 2), part_a(dz, dx), part_a(dz, dx), dev(dx=step))

    def b_along_z(dz, dx, step):
        to = (dz - step) % NZ
        send(("bz", to, dx), part_b(dz, dx), part_b(to, dx), dev(dz=step))

    def to_sibling(dz, dx):
        send(("cc", dz, dx), unit(dz, dx), unit(dz, dx), dev(dc=1))

    def right_hops(dx):
        return 4 if dx in (0, 1) else 3

    def b_round(k, dx):
        if k <= right_hops(dx):
            arrive(("bz", NZ - k, dx), part_b(NZ - k, dx))
            if k < right_hops(dx):
                b_along_z(NZ - k, dx, 1)
        if k <= 7 - right_hops(dx):
            arrive(("bz", k, dx), part_b(k, dx))
            if k < 7 - right_hops(dx):
                b_along_z(k, dx, -1)

    def eye():
        return (lax.broadcasted_iota(jnp.int32, (128, 128), 0)
                == lax.broadcasted_iota(jnp.int32, (128, 128), 1))

    def logits(g, n):
        rows = 2 * 128
        lo, hi = ((0, 512), (512, VD), (0, VD))[n]
        acc = jnp.zeros((rows, hi - lo), F32)
        for xi in range(NX):
            lhs = gat[2 * g:2 * g + 2, xi].reshape(rows, FQ)
            acc += lax.dot_general(
                lhs, wt[lo:hi, xi * FQ:(xi + 1) * FQ],
                (((1,), (1,)), ((), ())), preferred_element_type=F32)
        acc = acc * LOG2E
        if hi == VD:
            acc = jnp.concatenate([acc, jnp.full((rows, VP - VD), FAR, F32)], axis=1)
        lg[g * rows:(g + 1) * rows, lo:lo + acc.shape[1]] = acc

    def stats(g):
        rows = 2 * 128
        at = slice(g * rows, (g + 1) * rows)
        lanes = [slice(j * 128, (j + 1) * 128) for j in range(VP // 128)]
        top = lg[at, lanes[0]]
        for ln in lanes[1:]:
            top = jnp.maximum(top, lg[at, ln])
        top = jnp.broadcast_to(jnp.max(top, axis=1, keepdims=True), (rows, 128))
        total = jnp.zeros((rows, 128), F32)
        for ln in lanes:
            e = jnp.exp2(lg[at, ln] - top)
            total += e
            low = e.astype(BF16)
            for b in range(2 * NC * NY):
                i, cc, yy = b // (NC * NY), b // NY % NC, b % NY
                pr[yy, 2 * g + i, cc, :, ln] = low[b * ROWS_DEV:(b + 1) * ROWS_DEV]
        for i in range(2):
            for k in (2, 1, 3):
                s = 2 * g + i
                send(("ye", (-k) % NY, s), pr.at[(y + k) % NY, s], y_in.at[(-k) % NY, s], dev(dy=k))
        total = jnp.broadcast_to(jnp.sum(total, axis=1, keepdims=True), (rows, 128))
        for i in range(2):
            where = (z + DZ[2 * g + i]) % NZ
            for j, col in enumerate((top, total)):
                st_own[pl.ds(j * 8 + where, 1), :] = jnp.sum(
                    jnp.where(eye(), col[i * 128:(i + 1) * 128], 0.0), axis=0, keepdims=True)

    gat[0, x, c, y] = n4[y]
    for k in (0, 1, 3, 2):
        if k:
            arrive(("y", k), gat.at[0, x, c, (y - k) % NY])
        a_along_z(0, k, 1)
        a_along_z(0, k, -1)
    send(("bx", 2), part_b(0, 0), part_b(0, 0), dev(dx=2))
    send(("bx", 3), part_b(0, 0), part_b(0, 0), dev(dx=1))
    send(("bx", 1), part_b(0, 0), part_b(0, 0), dev(dx=-1))
    a_along_x(0)
    b_along_z(0, 0, 1)
    b_along_z(0, 0, -1)
    to_sibling(0, 0)

    for dx in (3, 1, 2):
        arrive(("bx", dx), part_b(0, dx))
        b_along_z(0, dx, 1)
        b_along_z(0, dx, -1)

    for k in (1, 3, 2):
        arrive(("sy", k), sh_y.at[k])
    sh_all[0, c] = sh_src[y] + sh_y[1] + sh_y[2] + sh_y[3]

    def finish_x(dz):
        for dx in range(1, NX):
            if dx == 2:
                arrive(("ax", dz, 2), part_a(dz, 2))
            to_sibling(dz, dx)

    def from_sibling(dz):
        for dx in range(NX):
            arrive(("cc", dz, dx), gat.at[SLOT[dz], (x + dx) % NX, 1 - c])

    def a_round(k):
        for p in (0, 1, 3, 2):
            arrive(("az", NZ - k, p), piece(NZ - k, p))
            if k < 4:
                a_along_z(NZ - k, p, 1)
                arrive(("az", k, p), piece(k, p))
                if k < 3:
                    a_along_z(k, p, -1)
        a_along_x(NZ - k)
        if k < 4:
            a_along_x(k)

    def b_all(k):
        for dx in range(NX):
            b_round(k, dx)

    def places(k):
        return {0: (0,), 4: (4,)}.get(k, (NZ - k, k))

    def opposite(k):
        for dz in places(k):
            a_opposite(dz)

    def finish(k):
        for dz in places(k):
            if dz:
                to_sibling(dz, 0)
            finish_x(dz)

    def shares_out():
        for dz in range(NZ):
            for dc in range(NC):
                if (dz, dc) != (0, 0):
                    send(("sz", (-dz) % NZ, dc), sh_all.at[0, c], sh_all.at[(-dz) % NZ, c],
                         dev(dz=dz, dc=dc))

    a_round(1)
    opposite(0)
    a_round(2)
    b_all(1)
    opposite(1)
    finish(0)
    a_round(3)
    opposite(2)
    b_all(2)
    finish(1)
    a_round(4)
    w_copy.wait()
    from_sibling(0)
    from_sibling(7)
    logits(0, 0)
    opposite(3)
    b_all(3)
    logits(0, 1)
    finish(2)
    stats(0)
    opposite(4)
    from_sibling(1)
    from_sibling(6)
    logits(1, 0)
    b_all(4)
    finish(3)
    finish(4)
    logits(1, 1)
    stats(1)
    from_sibling(2)
    from_sibling(5)
    logits(2, 2)
    stats(2)
    from_sibling(3)
    from_sibling(4)
    shares_out()
    logits(3, 2)
    stats(3)

    def merge(parts):
        top = parts[0][0]
        for m, _ in parts[1:]:
            top = jnp.maximum(top, m)
        total = jnp.zeros_like(top)
        for m, s in parts:
            total += s * jnp.exp2(m - top)
        return top, total

    near_peers = [(a, b) for a in range(NX) for b in range(NC) if (a, b) != (0, 0)]
    for a, b in near_peers:
        send(("tx", (-a) % NX, b), st_own, st_x.at[(-a) % NX, b], dev(dx=a, dc=b))
    parts = [(st_own[0:8], st_own[8:16])]
    for a, b in near_peers:
        arrive(("tx", a, b), st_x.at[a, b])
        parts.append((st_x[a, b, 0:8], st_x[a, b, 8:16]))
    top, total = merge(parts)
    st_zsrc[0:8] = top
    st_zsrc[8:16] = total
    for k in range(1, NZ):
        send(("tz", (-k) % NZ), st_zsrc, st_z.at[(-k) % NZ], dev(dz=k))
    parts = [(top, total)]
    for k in range(1, NZ):
        arrive(("tz", k), st_z.at[k])
        parts.append((st_z[k, 0:8], st_z[k, 8:16]))
    top, total = merge(parts)
    for dz in range(NZ):
        for dc in range(NC):
            if (dz, dc) != (0, 0):
                arrive(("sz", dz, dc), sh_all.at[dz, (c + dc) % NC])
        sh_abs[pl.ds((z + dz) % NZ, 1), :] = sh_all[dz, 0, 0:1] + sh_all[dz, 1, 0:1]
    f_own[...] = sh_abs[...] * jnp.exp2(st_own[0:8] - top) / total
    for k in (2, 1, 3):
        send(("yf", (-k) % NY), f_own, f_in.at[(-k) % NY], dev(dy=k))
    for k in range(1, NY):
        arrive(("yf", k), f_in.at[k])

    lane = lax.broadcasted_iota(jnp.int32, (NC * ROWS_DEV, 128), 1)
    row = lax.broadcasted_iota(jnp.int32, (NC * ROWS_DEV, 128), 0)
    take = lane == row // ROWS_DEV * 64 + y * ROWS_DEV + row % ROWS_DEV

    def mixing(s):
        dz = DZ[s]
        at = pl.ds((z + dz) % NZ, 1)
        for k in range(1, NY):
            arrive(("ye", k, s), y_in.at[k, s])
        cols = []
        for k in range(NY):
            factors = f_in[k, at, :] if k else f_own[at, :]
            col = jnp.sum(jnp.where(take, factors, 0.0), axis=1, keepdims=True)
            cols.append(jnp.broadcast_to(col, (NC * ROWS_DEV, 128)))
        for j in range(VP // 128):
            ln = slice(j * 128, (j + 1) * 128)
            mixed = pr[y, s, :, :, ln].reshape(NC * ROWS_DEV, 128).astype(F32) * cols[0]
            for k in range(1, NY):
                mixed += y_in[k, s, :, :, ln].reshape(NC * ROWS_DEV, 128).astype(F32) * cols[k]
            mix[s, :, :, ln] = mixed.astype(BF16).reshape(NC, ROWS_DEV, 128)
        for dc in range(NC):
            if (dz, dc) != (0, 0):
                send(("rz", (-dz) % NZ, dc), mix.at[s, (c + dc) % NC],
                     out_ref.at[z, c], dev(dz=dz, dc=dc))

    for dz in (4, 3, 5, 2, 6, 1, 7, 0):
        mixing(SLOT[dz])
    last = pltpu.make_async_copy(mix.at[0, c], out_ref.at[z, c], loc_sem)
    last.start()
    last.wait()
    for dz in range(NZ):
        for dc in range(NC):
            if (dz, dc) != (0, 0):
                arrive(("rz", dz, dc), out_ref.at[(z + dz) % NZ, (c + dc) % NC])
    for copy in sent:
        copy.wait_send()


def spread(mix_ref, out_ref):
    chunks = NZ * NC
    for j in range(chunks):
        start = j * VD
        base, shift = start // 128 * 128, start % 128
        vals = jnp.log(mix_ref[j // NC, j % NC].astype(F32))
        wide = jnp.concatenate([vals, jnp.zeros((ROWS_DEV, 128), F32)], axis=1)
        if shift:
            wide = pltpu.roll(wide, shift, 1)
            lane = lax.broadcasted_iota(jnp.int32, (ROWS_DEV, 128), 1)
            first = jnp.where(lane < shift, out_ref[:, base:base + 128], wide[:, 0:128])
            out_ref[:, base:base + 128] = first
        else:
            out_ref[:, base:base + 128] = wide[:, 0:128]
        end = min(base + wide.shape[1], chunks * VD)
        out_ref[:, base + 128:end] = wide[:, 128:end - base]


def per_device(hidden, norm_gain, head_weight, expert_ids, mix_weight):
    wt_in = jnp.transpose(head_weight.reshape(D, VD))
    vmem = pl.BlockSpec(memory_space=pltpu.VMEM)
    n_sem = len(SEMS)
    returned = pl.pallas_call(
        body,
        out_shape=jax.ShapeDtypeStruct((NZ, NC, ROWS_DEV, VP), BF16),
        in_specs=[vmem, vmem, vmem, vmem, pl.BlockSpec(memory_space=pl.ANY)],
        out_specs=vmem,
        scratch_shapes=[
            pltpu.VMEM((VD, D), BF16),
            pltpu.VMEM((NY, ROWS_DEV, FQ), BF16),
            pltpu.VMEM((NZ, NX, NC, NY, ROWS_DEV, FQ), BF16),
            pltpu.VMEM((8, 128), F32),
            pltpu.VMEM((NY, 8, 128), F32),
            pltpu.VMEM((NY, 8, 128), F32),
            pltpu.VMEM((NZ, NC, 8, 128), F32),
            pltpu.VMEM((NZ * 128, VP), F32),
            pltpu.VMEM((16, 128), F32),
            pltpu.VMEM((NX, NC, 16, 128), F32),
            pltpu.VMEM((16, 128), F32),
            pltpu.VMEM((NZ, 16, 128), F32),
            pltpu.VMEM((8, 128), F32),
            pltpu.VMEM((8, 128), F32),
            pltpu.VMEM((NY, 8, 128), F32),
            pltpu.VMEM((NY, NZ, NC, ROWS_DEV, VP), BF16),
            pltpu.VMEM((NY, NZ, NC, ROWS_DEV, VP), BF16),
            pltpu.VMEM((NZ, NC, ROWS_DEV, VP), BF16),
            pltpu.SemaphoreType.DMA,
            pltpu.SemaphoreType.DMA,
            pltpu.SemaphoreType.DMA((n_sem,)),
            pltpu.SemaphoreType.DMA((n_sem,)),
        ],
        compiler_params=pltpu.CompilerParams(
            collective_id=0, has_side_effects=True, vmem_limit_bytes=56 * 1024 * 1024),
    )(hidden, norm_gain, expert_ids.T, mix_weight.T, wt_in)
    return pl.pallas_call(
        spread,
        out_shape=jax.ShapeDtypeStruct((ROWS_DEV, NZ * NC * VD), F32),
        in_specs=[vmem],
        out_specs=vmem,
    )(returned)


def solution(mesh):
    placed = (
        P("expert", None),
        P(),
        P(None, "tensor", "expert"),
        P("expert", None),
        P("expert", None),
    )
    return jax.shard_map(
        per_device, mesh=mesh, in_specs=placed, out_specs=P("expert", "tensor"), check_vma=False
    )
```
